128 devices in a mesh: dp: 8 (over z, x_hi), mp: 16 (over y, x_lo, core).
Axes of the slice: x: 4 (x_hi: 2, x_lo: 2; x = x_hi * 2 + x_lo), y: 4, z: 4, core: 2. Of those that a mesh axis runs over, the one named last changes fastest.
Arguments:
- block_input_tokens: bfloat16 [6144, 3072], P(('dp', 'mp')), may hold values from -6 to 6
- norm_gain_vector: float32 [3072], replicated, may hold values from 0.5 to 1.5
- w_in: bfloat16 [3072, 24576], P(None, 'mp'), may hold values from -0.109375 to 0.109375
- w_out: bfloat16 [16384, 3072], P('mp'), may hold values from -0.046875 to 0.046875
- saved_qkv: bfloat16 [6144, 12288], P('dp', 'mp'), may hold values from -46 to 46
- mlp_pre: bfloat16 [6144, 12288], P('dp', 'mp'), may hold values from -6 to 6
- output_gradient: bfloat16 [6144, 3072], P(('dp', 'mp')), may hold values from -24 to 24
Outputs:
- input_gradient: bfloat16 [6144, 3072], P(('dp', 'mp'))
- grad_w_in: float32 [3072, 24576], P('dp', 'mp')
- grad_w_out: float32 [16384, 3072], P('mp', 'dp')
The draws below stay inside these ranges and needn't reach their ends.
All inputs are finite; a program needn't handle non-finite values.
Results may differ from the reference program's by a relative error of at most 0.025.
Values may be sent and summed in bfloat16 or wider, within the bound.
A program may use at most 192 MiB of HBM per device.

```python
import jax
import jax.numpy as jnp
from jax import lax

D = 3072
HD = 128
HEADS_DEV = 2
FF_DEV = 768
PATCHES = 256
ATT_DEV = 256
IN_DEV = 1536
OUT_DEV = 1024
TOKENS = 6144
N_MP = 16


def draw_saved_qkv(key, part):
    key = jax.random.fold_in(key, 11)
    shape = (TOKENS // PATCHES, PATCHES, N_MP, 3, HEADS_DEV, HD)
    base = jnp.clip(jax.random.normal(key, shape, jnp.float32), -6.0, 6.0)
    return base.reshape(TOKENS, N_MP * 3 * ATT_DEV).astype(jnp.bfloat16)


def strengthened(entries, key, source, target, blocks, factor):
    owner, partner = [(jnp.arange(entries.shape[axis_at]) // (entries.shape[axis_at] // blocks)).reshape([-1 if axis == axis_at else 1 for axis in range(entries.ndim)]) for axis_at in (source, target)]
    chosen = jax.random.permutation(key, blocks)[partner]
    strong = (owner == chosen) | (owner == (partner + blocks // 2) % blocks)
    return jnp.where(strong, factor * entries, entries)


def level_of(stream_key, dims, cuts, low, high):
    def one(position, shards_of):
        steps = jax.random.uniform(jax.random.fold_in(jax.random.fold_in(stream_key, 6), position), (shards_of,), jnp.float32, low / len(cuts), high / len(cuts))
        return jnp.repeat(jnp.exp(steps), dims[position] // shards_of).reshape((-1,) + (1,) * (len(dims) - position - 1))

    loudness = one(*cuts[0])
    for cut in cuts[1:]:
        loudness = loudness * one(*cut)
    return loudness


def gaussian(own_key, dims, scale, reach, pieces=(), kind=jnp.bfloat16):
    entries = scale * jax.random.normal(own_key, dims, jnp.float32)
    if pieces:
        entries = entries * level_of(own_key, dims, pieces, -0.22, 0.18)
    return jnp.clip(entries, -reach, reach).astype(kind)


def bell_draw_with(stream_key, extent, scale, reach, shards, heavy, held_as=jnp.bfloat16):
    values = scale * jax.random.normal(stream_key, extent, jnp.float32)
    if shards:
        values = values * level_of(stream_key, extent, shards, -0.22, 0.18)
    return jnp.clip(strengthened(values, jax.random.fold_in(stream_key, 3), *heavy), -reach, reach).astype(held_as)


def setup_inputs(seed: int = 0) -> dict:
    seeds = jax.random.split(jax.random.key(seed), 8)
    return {
        "block_input_tokens": gaussian(seeds[0], (TOKENS, D), 1.0, 6.0, ((0, 128),)),
        "norm_gain_vector": jnp.clip(1.0 + 0.1 * jax.random.normal(seeds[1], (D,), jnp.float32), 0.5, 1.5),
        "w_in": gaussian(seeds[2], (D, N_MP * IN_DEV), D ** -0.5, 0.109375, ((1, 16),)),
        "w_out": gaussian(seeds[3], (N_MP * OUT_DEV, D), (N_MP * OUT_DEV) ** -0.5, 0.046875, ((0, 16),)),
        "saved_qkv": draw_saved_qkv(jax.random.fold_in(seeds[7], 71), 0),
        "mlp_pre": gaussian(seeds[5], (TOKENS, N_MP * FF_DEV), 1.0, 6.0, ((0, 8), (1, 16))),
        "output_gradient": bell_draw_with(seeds[6], (TOKENS, D), 1.0, 24.0, ((0, 128),), (0, 1, 128, 5.5)),
    }


def layer_statistics(block_input_tokens):
    values = block_input_tokens.astype(jnp.float32)
    center = lax.optimization_barrier(jnp.mean(values, axis=-1, keepdims=True))
    spread = lax.optimization_barrier(jnp.mean((values - center) ** 2, axis=-1, keepdims=True))
    inverse_deviation = 1.0 / jnp.sqrt(spread + 1e-06)
    return ((values - center) * inverse_deviation, inverse_deviation)

def gelu_slope(pre):
    cumul = 0.5 * (1.0 + jax.scipy.special.erf(pre * 0.7071067811865476))
    dens = jnp.exp(-0.5 * pre * pre) * 0.3989422804014327
    return cumul + pre * dens

def reference(block_input_tokens, norm_gain_vector, w_in, w_out, saved_qkv, mlp_pre, output_gradient):
    scale = HD ** (-0.5)
    images_all = TOKENS // PATCHES
    heads_all = N_MP * HEADS_DEV
    centered_standardized, inverse_deviation = layer_statistics(block_input_tokens)
    normalized_tokens = (centered_standardized * norm_gain_vector).astype(jnp.bfloat16)
    split = saved_qkv.reshape(TOKENS, N_MP, 3, HEADS_DEV, HD)
    queries = split[:, :, 0].reshape(images_all, PATCHES, heads_all, HD)
    keys = split[:, :, 1].reshape(images_all, PATCHES, heads_all, HD)
    values = split[:, :, 2].reshape(images_all, PATCHES, heads_all, HD)
    qf = queries.astype(jnp.float32)
    kf = keys.astype(jnp.float32)
    vf = values.astype(jnp.float32)
    scores = jnp.einsum('bqhd,bkhd->bhqk', qf, kf) * scale
    probs_f = jax.nn.softmax(scores, axis=-1)
    probs = probs_f.astype(jnp.bfloat16)
    heads_out = jnp.einsum('bhqk,bkhd->bqhd', probs.astype(jnp.float32), vf).astype(jnp.bfloat16)
    pre = mlp_pre.astype(jnp.float32)
    act = jax.nn.gelu(pre, approximate=False).astype(jnp.bfloat16)
    joined = jnp.concatenate([heads_out.reshape(TOKENS, N_MP, ATT_DEV), act.reshape(TOKENS, N_MP, FF_DEV)], axis=2)
    joined = joined.reshape(TOKENS, N_MP * OUT_DEV)
    grad_joined = jnp.dot(output_gradient, w_out.T, preferred_element_type=jnp.float32).astype(jnp.bfloat16)
    grad_w_out = jnp.dot(joined.T, output_gradient, preferred_element_type=jnp.float32)
    grad_split = grad_joined.reshape(TOKENS, N_MP, OUT_DEV)
    grad_heads = grad_split[:, :, :ATT_DEV].reshape(images_all, PATCHES, heads_all, HD)
    grad_act = grad_split[:, :, ATT_DEV:].reshape(TOKENS, N_MP * FF_DEV)
    ghf = grad_heads.astype(jnp.float32)
    grad_v = jnp.einsum('bhqk,bqhd->bkhd', probs.astype(jnp.float32), ghf).astype(jnp.bfloat16)
    grad_probs = jnp.einsum('bqhd,bkhd->bhqk', ghf, vf)
    delta = lax.optimization_barrier(jnp.sum(ghf * heads_out.astype(jnp.float32), axis=-1))
    delta = jnp.transpose(delta, (0, 2, 1))[..., None]
    grad_scores = (probs_f * (grad_probs - delta) * scale).astype(jnp.bfloat16)
    gsf = grad_scores.astype(jnp.float32)
    grad_q = jnp.einsum('bhqk,bkhd->bqhd', gsf, kf).astype(jnp.bfloat16)
    grad_k = jnp.einsum('bhqk,bqhd->bkhd', gsf, qf).astype(jnp.bfloat16)
    grad_pre = (grad_act.astype(jnp.float32) * gelu_slope(pre)).astype(jnp.bfloat16)
    grad_proj = jnp.concatenate([grad_q.reshape(TOKENS, N_MP, ATT_DEV), grad_k.reshape(TOKENS, N_MP, ATT_DEV), grad_v.reshape(TOKENS, N_MP, ATT_DEV), grad_pre.reshape(TOKENS, N_MP, FF_DEV)], axis=2)
    grad_w_in = jnp.dot(normalized_tokens.T, grad_proj.reshape(TOKENS, N_MP * IN_DEV), preferred_element_type=jnp.float32)
    proj_blocks = jnp.transpose(grad_proj, (1, 0, 2))
    weight_blocks = jnp.transpose(w_in.reshape(D, N_MP, IN_DEV), (1, 0, 2))

    def add_block(total, pair):
        partial_sum = jnp.dot(pair[0], pair[1].T, preferred_element_type=jnp.float32)
        rounded = lax.optimization_barrier(partial_sum.astype(jnp.bfloat16))
        return (total + rounded.astype(jnp.float32), None)
    grad_normed, unused = lax.scan(add_block, jnp.zeros((TOKENS, D), jnp.float32), (proj_blocks, weight_blocks))
    scaled_gradient = grad_normed * norm_gain_vector
    first_moment = lax.optimization_barrier(jnp.mean(scaled_gradient, axis=-1, keepdims=True))
    second_moment = lax.optimization_barrier(jnp.mean(scaled_gradient * centered_standardized, axis=-1, keepdims=True))
    input_gradient = output_gradient.astype(jnp.float32) + (scaled_gradient - first_moment - centered_standardized * second_moment) * inverse_deviation
    return (input_gradient.astype(jnp.bfloat16), grad_w_in, grad_w_out)
```

```python
import functools

import jax
import jax.numpy as jnp
from jax import lax
from jax.experimental import pallas as pl
from jax.experimental.pallas import tpu as pltpu
from jax.sharding import PartitionSpec as P

HD = 128
F32 = jnp.float32
BF16 = jnp.bfloat16
SCALE = HD ** (-0.5)
MESH = pl.DeviceIdType.MESH
NSO = 2
NSI = 4
HO = 1024 // NSO // 2
HI = 384 // NSI // 2


def nt(a, b):
    return lax.dot_general(a, b, (((1,), (1,)), ((), ())), preferred_element_type=F32)


def nn(a, b):
    return lax.dot_general(a, b, (((1,), (0,)), ((), ())), preferred_element_type=F32)


def tn(a, b):
    return lax.dot_general(a, b, (((0,), (0,)), ((), ())), preferred_element_type=F32)


def loop(n, fn):
    def step(i, carry):
        fn(i)
        return carry

    lax.fori_loop(0, n, step, 0)


def al(v, m):
    return pl.multiple_of(v, m)


def kernel(
    tok, gain, win, wout, qkv_hbm, pre_hbm, dout,
    ig, gwin, gwout,
    buf_a, buf_b, qkv, pre, slope, pf, heads, joined_t, gh, gproj, wslot, cout, cin,
    rzo, rzi, rxo, rxi, rs_sib, rs_y, rs_x, ss_x, xhat, gn, own_tok, own_dout, rstd_ref,
    lsem, ag_s, ag_r, zo_s, zo_r, zi_s, zi_r, xo_s, xo_r, xi_s, xi_r, ms_s, ms_r,
    my_s, my_r, mx_s, mx_r,
):
    dp = lax.axis_index("dp")
    mp = lax.axis_index("mp")
    z = dp // 2
    xh = dp % 2
    y = mp // 4
    xl = (mp // 2) % 2
    c = mp % 2
    zp, zm, z2 = (z + 1) % 4, (z + 3) % 4, (z + 2) % 4
    yp, ym, y2 = (y + 1) % 4, (y + 3) % 4, (y + 2) % 4
    xn, cn, xo = 1 - xl, 1 - c, 1 - xh

    def m_of(yy, xx, cc):
        return yy * 4 + xx * 2 + cc

    d_sib = (dp, m_of(y, xl, cn))
    d_xn = (dp, m_of(y, xn, c))
    d_yp = (dp, m_of(yp, xl, c))
    d_ym = (dp, m_of(ym, xl, c))
    d_y2 = (dp, m_of(y2, xl, c))
    d_zp = (zp * 2 + xh, mp)
    d_zm = (zm * 2 + xh, mp)
    d_xo = (z * 2 + xo, mp)
    friends = (d_sib, d_xn, d_yp, d_ym, d_y2, d_zp, d_zm, d_xo)

    def load(src, dst, i):
        return pltpu.make_async_copy(src, dst, lsem.at[i])

    l_dout = load(dout, own_dout, 0)
    l_tok = load(tok, own_tok, 1)
    l_qkv = load(qkv_hbm, qkv, 2)
    l_pre = load(pre_hbm, pre, 3)
    for l in (l_dout, l_tok, l_qkv, l_pre):
        l.start()

    def wout_loads(nb, row):
        return [
            load(
                wout.at[pl.ds(nb * 256, 256), pl.ds(h * 1536, 1536)],
                wslot.at[pl.ds(row + h * 256, 256)],
                4 + nb * 2 + h,
            )
            for h in range(2)
        ]

    wo_rows = (0, 512, 1024, 0)
    wo_loads = [wout_loads(nb, wo_rows[nb]) for nb in range(4)]
    for nb in range(3):
        for l in wo_loads[nb]:
            l.start()

    barrier = pltpu.get_barrier_semaphore()
    for d in friends:
        pl.semaphore_signal(barrier, inc=1, device_id=d, device_id_type=MESH)
    pl.semaphore_wait(barrier, len(friends))

    def remote(src, dst, s, r, d):
        return pltpu.make_async_remote_copy(
            src_ref=src, dst_ref=dst, send_sem=s, recv_sem=r, device_id=d, device_id_type=MESH
        )

    order = (z2, zp, zm, z)
    me = m_of(y, xl, c)
    mx = m_of(y, xn, c)
    ag_out = (
        (me, d_sib), (me, d_xn), (me, d_yp), (me, d_ym), (me, d_y2),
        (mx, d_yp), (mx, d_ym), (mx, d_y2), (mx, d_sib),
        (m_of(ym, xl, c), d_sib), (m_of(yp, xl, c), d_sib), (m_of(y2, xl, c), d_sib),
        (m_of(ym, xn, c), d_sib), (m_of(yp, xn, c), d_sib), (m_of(y2, xn, c), d_sib),
    )
    ag_in = (
        m_of(y, xl, cn), mx, m_of(ym, xl, c), m_of(yp, xl, c), m_of(y2, xl, c),
        m_of(ym, xn, c), m_of(yp, xn, c), m_of(y2, xn, c), m_of(y, xn, cn),
        m_of(ym, xl, cn), m_of(yp, xl, cn), m_of(y2, xl, cn),
        m_of(ym, xn, cn), m_of(yp, xn, cn), m_of(y2, xn, cn),
    )
    bufs = (buf_a, buf_b)

    def block(w, o, m):
        return bufs[w].at[order[o], pl.ds(al(m * 48, 16), 48), :]

    def ag_send(w, o, ts):
        for t in ts:
            m, d = ag_out[t]
            b = block(w, o, m)
            remote(b, b, ag_s.at[w, o, t], ag_r.at[w, o, t], d).start()

    def ag_wait(w, o, ts):
        for t in ts:
            b = block(w, o, ag_in[t])
            remote(b, b, ag_s.at[w, o, t], ag_r.at[w, o, t], ag_out[t][1]).wait_recv()

    def ag_start(w, o):
        ag_send(w, o, (1, 2, 3, 4, 0))

    def ag_x(w, o):
        ag_wait(w, o, (1,))
        ag_send(w, o, (5, 6, 7, 8))

    def ag_y(w, o):
        ag_wait(w, o, (2, 3, 4))
        ag_send(w, o, (9, 10, 11))

    def ag_yx(w, o):
        ag_wait(w, o, (5, 6, 7))
        ag_send(w, o, (12, 13, 14))

    def ag_sib(w, o):
        ag_wait(w, o, (0, 8, 9, 10, 11, 12, 13, 14))

    def ag_drain(w):
        for o in range(4):
            for t in range(15):
                m, d = ag_out[t]
                b = block(w, o, m)
                remote(b, b, ag_s.at[w, o, t], ag_r.at[w, o, t], d).wait_send()

    l_dout.wait()
    for o in range(4):
        buf_a[order[o], pl.ds(al(me * 48, 16), 48), :] = own_dout[
            :, pl.ds(al(order[o] * 768, 128), 768)
        ]
        if o < 2:
            ag_start(0, o)

    l_tok.wait()
    x = own_tok[...].astype(F32)
    center = jnp.mean(x, axis=-1, keepdims=True)
    spread = jnp.mean((x - center) ** 2, axis=-1, keepdims=True)
    rstd = 1.0 / jnp.sqrt(spread + 1e-06)
    xhat[...] = (x - center) * rstd
    rstd_ref[...] = jnp.broadcast_to(rstd, rstd_ref.shape)
    for o in range(4):
        buf_b[o, pl.ds(al(me * 48, 16), 48), :] = (
            xhat[:, pl.ds(o * 768, 768)] * gain[:, pl.ds(o * 768, 768)]
        ).astype(BF16)

    def att_fwd(b):
        rows = pl.ds(b * 256, 256)
        for h in range(2):
            q = qkv[rows, pl.ds(h * 128, 128)]
            k = qkv[rows, pl.ds(256 + h * 128, 128)]
            v = qkv[rows, pl.ds(512 + h * 128, 128)]
            s = nt(q, k) * SCALE
            e = jnp.exp(s - jnp.max(s, axis=-1, keepdims=True))
            p = e / jnp.sum(e, axis=-1, keepdims=True)
            pf[b * 2 + h] = p
            out = nn(p.astype(BF16), v)
            heads[rows, pl.ds(h * 128, 128)] = out.astype(BF16)
            joined_t[pl.ds(h * 128, 128), rows] = jnp.transpose(out).astype(BF16)

    def gelu(t):
        rows = pl.ds(al(t * 128, 128), 128)
        v = pre[rows, :].astype(F32)
        cumul = 0.5 * (1.0 + lax.erf(v * 0.7071067811865476))
        joined_t[pl.ds(256, 768), rows] = jnp.transpose(v * cumul).astype(BF16)
        dens = jnp.exp(-0.5 * v * v) * 0.3989422804014327
        slope[rows, :] = cumul + v * dens

    l_qkv.wait()
    att_fwd(0)
    ag_x(0, 0)
    ag_start(0, 2)
    att_fwd(1)
    ag_x(0, 1)
    ag_start(0, 3)
    att_fwd(2)
    ag_y(0, 0)
    ag_x(0, 2)
    l_pre.wait()
    gelu(0)
    gelu(1)
    ag_yx(0, 0)
    ag_x(0, 3)
    gelu(2)
    gelu(3)
    ag_y(0, 1)
    ag_yx(0, 1)
    gelu(4)
    gelu(5)
    ag_sib(0, 0)
    ag_y(0, 2)

    class Ring:
        def __init__(self, src, rbuf, ssem, rsem, add):
            self.src, self.rbuf, self.ssem, self.rsem, self.add = src, rbuf, ssem, rsem, add
            self.sent = []

        def send(self, i, src, d):
            cp = remote(src, self.rbuf.at[i], self.ssem.at[i], self.rsem.at[i], d)
            cp.start()
            self.sent.append(cp)

        def wait(self, i):
            b = self.rbuf.at[i]
            remote(b, b, self.ssem.at[i], self.rsem.at[i], d_zp).wait_recv()

        def far(self):
            self.send(0, self.src(z2, 1), d_zp)
            self.send(1, self.src(z2, 0), d_zm)

        def near_p(self):
            self.send(2, self.src(zp, 0), d_zp)

        def near_m(self):
            self.send(3, self.src(zm, 1), d_zm)

        def relay_p(self):
            self.wait(0)
            self.add(self.rbuf.at[0], self.src(zp, 1))
            self.send(4, self.rbuf.at[0], d_zp)

        def relay_m(self):
            self.wait(1)
            self.add(self.rbuf.at[1], self.src(zm, 0))
            self.send(5, self.rbuf.at[1], d_zm)

        def arrived(self):
            for i in (2, 3, 4, 5):
                self.wait(i)

        def drain(self):
            for cp in self.sent:
                cp.wait_send()

    def add_o(dst, src):
        def step(i):
            rows = pl.ds(al(i * 64, 64), 64)
            for h in range(2):
                dst[h, rows, :] = (
                    dst[h, rows, :].astype(F32) + src[h, rows, :].astype(F32)
                ).astype(BF16)

        loop(HO // 64, step)

    def add_i(dst, src):
        def step(i):
            rows = pl.ds(al(i * 16, 16), 16)
            for h in range(2):
                dst[h, rows, :] = (
                    dst[h, rows, :].astype(F32) + src[h, rows, :].astype(F32)
                ).astype(BF16)

        loop(HI // 16, step)

    def src_o(s):
        return lambda zz, half: cout.at[
            pl.ds(zz * 2, 2), pl.ds(s * 2 * HO + half * HO, HO), :
        ]

    def src_i(s):
        return lambda zz, half: cin.at[
            pl.ds(zz * 2, 2), pl.ds(s * 2 * HI + half * HI, HI), :
        ]

    ro = [Ring(src_o(s), rzo.at[s], zo_s.at[s], zo_r.at[s], add_o) for s in range(NSO)]
    ri = [Ring(src_i(s), rzi.at[s], zi_s.at[s], zi_r.at[s], add_i) for s in range(NSI)]

    class Cross:
        def __init__(self, ring, part, rx, out, ssem, rsem, base, height, tile):
            self.ring, self.part, self.rx, self.out = ring, part, rx, out
            self.ssem, self.rsem = ssem, rsem
            self.base, self.height, self.tile = base, height, tile
            self.sent = []

        def send(self):
            self.ring.arrived()
            r = self.ring.rbuf
            for half, (a, b) in enumerate(((2, 5), (3, 4))):
                off = self.base + half * self.height

                def step(i, a=a, b=b, off=off):
                    rows = pl.ds(al(i * self.tile, self.tile), self.tile)
                    prow = pl.ds(al(off + i * self.tile, self.tile), self.tile)
                    r[a, xo, rows, :] = (
                        r[a, xo, rows, :].astype(F32)
                        + r[b, xo, rows, :].astype(F32)
                        + self.part[z * 2 + xo, prow, :].astype(F32)
                    ).astype(BF16)

                loop(self.height // self.tile, step)
                cp = remote(
                    r.at[a, xo], self.rx.at[pl.ds(off, self.height), :],
                    self.ssem.at[half], self.rsem.at[half], d_xo,
                )
                cp.start()
                self.sent.append(cp)

        def finish(self):
            r = self.ring.rbuf
            for half, (a, b) in enumerate(((2, 5), (3, 4))):
                off = self.base + half * self.height
                dst = self.rx.at[pl.ds(off, self.height), :]
                remote(dst, dst, self.ssem.at[half], self.rsem.at[half], d_xo).wait_recv()

                def step(i, a=a, b=b, off=off):
                    rows = pl.ds(al(i * self.tile, self.tile), self.tile)
                    prow = pl.ds(al(off + i * self.tile, self.tile), self.tile)
                    self.rx[prow, :] = (
                        r[a, xh, rows, :].astype(F32)
                        + r[b, xh, rows, :].astype(F32)
                        + self.part[z * 2 + xh, prow, :].astype(F32)
                        + self.rx[prow, :].astype(F32)
                    ).astype(BF16)

                loop(self.height // self.tile, step)

        def drain(self):
            for cp in self.sent:
                cp.wait_send()

    co = [
        Cross(ro[s], cout, rxo, gwout, xo_s.at[s], xo_r.at[s], s * 2 * HO, HO, 64)
        for s in range(NSO)
    ]
    ci = [
        Cross(ri[s], cin, rxi, gwin, xi_s.at[s], xi_r.at[s], s * 2 * HI, HI, 16)
        for s in range(NSI)
    ]

    def out_chunk(o):
        j = order[o]

        def step(r):
            rows = pl.ds(al(r * 256, 256), 256)
            t = nn(joined_t[rows, :], buf_a[j]).astype(BF16)
            cout[j * 2, rows, :] = t[:, :384]
            cout[j * 2 + 1, rows, :] = t[:, 384:]

        loop(4, step)

    out_chunk(0)
    for r in ro:
        r.far()
    ag_yx(0, 2)
    ag_sib(0, 1)
    ag_y(0, 3)
    out_chunk(1)
    for r in ro:
        r.near_p()
    ag_yx(0, 3)
    ag_sib(0, 2)
    out_chunk(2)
    for r in ro:
        r.near_m()
    ag_start(1, 0)
    ag_start(1, 1)
    ag_sib(0, 3)
    out_chunk(3)
    ag_x(1, 0)
    ag_x(1, 1)
    ag_start(1, 2)
    ag_start(1, 3)

    def joined_grad(nb):
        for l in wo_loads[nb]:
            l.wait()
        row = wo_rows[nb]

        def step(r):
            rows = pl.ds(al(r * 384, 128), 384)
            acc = jnp.zeros((384, 256), F32)
            for j in range(4):
                w = wslot[pl.ds(row + (j // 2) * 256, 256), pl.ds((j % 2) * 768, 768)]
                acc = acc + nt(buf_a[j, rows, :], w)
            g = acc.astype(BF16)
            if nb == 0:
                gh[rows, :] = g
            else:
                cols = pl.ds((nb - 1) * 256, 256)
                gproj[rows, pl.ds(768 + (nb - 1) * 256, 256)] = (
                    g.astype(F32) * slope[rows, cols]
                ).astype(BF16)

        loop(2, step)

    joined_grad(0)
    for l in wo_loads[3]:
        l.start()
    ro[0].relay_p()
    ro[0].relay_m()
    ag_x(1, 2)
    ag_x(1, 3)
    joined_grad(1)
    ag_y(1, 0)
    ag_y(1, 1)
    joined_grad(2)
    ag_yx(1, 0)
    ag_yx(1, 1)
    joined_grad(3)
    ag_y(1, 2)
    ag_y(1, 3)
    ro[1].relay_p()
    ro[1].relay_m()

    def win_load(j):
        return load(
            win.at[pl.ds(j * 768, 768), :], wslot.at[pl.ds((j % 2) * 768, 768)], 12 + j
        )

    win_load(0).start()
    win_load(1).start()

    def att_bwd(b):
        rows = pl.ds(b * 256, 256)
        for h in range(2):
            q = qkv[rows, pl.ds(h * 128, 128)]
            k = qkv[rows, pl.ds(256 + h * 128, 128)]
            v = qkv[rows, pl.ds(512 + h * 128, 128)]
            g = gh[rows, pl.ds(h * 128, 128)]
            p = pf[b * 2 + h]
            delta = jnp.sum(
                g.astype(F32) * heads[rows, pl.ds(h * 128, 128)].astype(F32),
                axis=-1, keepdims=True,
            )
            ds = (p * (nt(g, v) - delta) * SCALE).astype(BF16)
            gproj[rows, pl.ds(512 + h * 128, 128)] = tn(p.astype(BF16), g).astype(BF16)
            gproj[rows, pl.ds(h * 128, 128)] = nn(ds, k).astype(BF16)
            gproj[rows, pl.ds(256 + h * 128, 128)] = tn(ds, q).astype(BF16)

    att_bwd(0)
    ag_yx(1, 2)
    ag_yx(1, 3)
    att_bwd(1)
    att_bwd(2)

    ag_drain(0)

    def transposed(o):
        ag_sib(1, o)
        j = order[o]

        def step(i):
            rows = pl.ds(al(i * 128, 128), 128)
            buf_a[j, :, rows] = jnp.transpose(buf_b[j, rows, :])

        loop(6, step)

    def in_chunk(o):
        j = order[o]

        def step(i):
            h, n = i // 2, i % 2
            rows = pl.ds(al(h * 384, 128), 384)
            cols = pl.ds(al(n * 768, 128), 768)
            cin[j * 2 + h, :, cols] = nn(buf_a[j, rows, :], gproj[:, cols]).astype(BF16)

        loop(4, step)

    transposed(0)
    in_chunk(0)
    for r in ri:
        r.far()
    transposed(1)
    in_chunk(1)
    for r in ri:
        r.near_p()
    transposed(2)
    in_chunk(2)
    for r in ri:
        r.near_m()
    transposed(3)
    in_chunk(3)
    co[0].send()
    co[1].send()
    ag_drain(1)

    def sib_copy(j):
        return remote(
            buf_b.at[j, pl.ds(al(cn * 384, 128), 384), :], rs_sib.at[j],
            ms_s.at[j], ms_r.at[j], d_sib,
        )

    def normed_grad(j):
        win_load(j).wait()
        base = (j % 2) * 768

        def step(i):
            h, n = i // 3, i % 3
            rows = pl.ds(al(h * 384, 128), 384)
            w = wslot[pl.ds(al(base + n * 256, 256), 256), :]
            t = nt(gproj[rows, :], w).astype(BF16)
            cols = pl.ds(al(n * 256, 128), 256)
            for b in range(8):
                buf_b[j, pl.ds(al((b % 2) * 384 + (h * 4 + b // 2) * 48, 16), 48), cols] = t[
                    b * 48 : b * 48 + 48
                ]

        loop(6, step)
        sib_copy(j).start()
        if j < 2:
            win_load(j + 2).start()

    y_rows = {0: yp, 1: ym, 2: y2}
    y_dev = (d_yp, d_ym, d_y2)

    def y_copy(j, i):
        return remote(
            buf_b.at[j, pl.ds(al(c * 384 + y_rows[i] * 96, 16), 96), :], rs_y.at[i, j],
            my_s.at[i, j], my_r.at[i, j], y_dev[i],
        )

    def sib_sum(j):
        sib_copy(j).wait_recv()

        def step(i):
            rows = pl.ds(al(c * 384 + i * 48, 16), 48)
            buf_b[j, rows, :] = (
                buf_b[j, rows, :].astype(F32)
                + rs_sib[j, pl.ds(al(i * 48, 16), 48), :].astype(F32)
            ).astype(BF16)

        loop(8, step)
        for i in range(3):
            y_copy(j, i).start()

    def x_copy(j):
        return remote(ss_x.at[j], rs_x.at[j], mx_s.at[j], mx_r.at[j], d_xn)

    def y_sum(j):
        for i in range(3):
            y_copy(j, i).wait_recv()

        def total(side):
            acc = buf_b[j, pl.ds(al(c * 384 + y * 96 + side * 48, 16), 48), :].astype(F32)
            for i in range(3):
                acc = acc + rs_y[i, j, pl.ds(al(side * 48, 16), 48), :].astype(F32)
            return acc

        ss_x[j] = total(xn).astype(BF16)
        x_copy(j).start()
        gn[:, pl.ds(j * 768, 768)] = total(xl)

    def x_sum(j):
        x_copy(j).wait_recv()
        cols = pl.ds(j * 768, 768)
        gn[:, cols] = gn[:, cols] + rs_x[j].astype(F32)

    normed_grad(0)
    ri[0].relay_p()
    ri[0].relay_m()
    normed_grad(1)
    sib_sum(0)
    normed_grad(2)
    sib_sum(1)
    ri[1].relay_p()
    ri[1].relay_m()
    normed_grad(3)
    sib_sum(2)
    co[0].finish()
    co[1].finish()
    st_o = load(rxo, gwout, 0)
    st_o.start()
    sib_sum(3)
    y_sum(0)
    ri[2].relay_p()
    ri[2].relay_m()
    y_sum(1)
    y_sum(2)
    y_sum(3)
    ri[3].relay_p()
    ri[3].relay_m()
    for j in range(4):
        x_sum(j)
    xh_v = xhat[...]
    sg = gn[...] * gain[...]
    m1 = jnp.mean(sg, axis=-1, keepdims=True)
    m2 = jnp.mean(sg * xh_v, axis=-1, keepdims=True)
    own_tok[...] = (
        own_dout[...].astype(F32) + (sg - m1 - xh_v * m2) * rstd_ref[:, :1]
    ).astype(BF16)
    st_g = load(own_tok, ig, 1)
    st_g.start()
    for s in range(NSI):
        ci[s].send()
    for s in range(NSI):
        ci[s].finish()
    st_i = load(rxi, gwin, 2)
    st_i.start()
    for r in ro + ri + co + ci:
        r.drain()
    for j in range(4):
        sib_copy(j).wait_send()
        x_copy(j).wait_send()
        for i in range(3):
            y_copy(j, i).wait_send()
    st_o.wait()
    st_g.wait()
    st_i.wait()


def body(block_input_tokens, norm_gain_vector, w_in, w_out, saved_qkv, mlp_pre, output_gradient):
    hbm = pl.BlockSpec(memory_space=pl.ANY)
    vmem = pl.BlockSpec(memory_space=pltpu.VMEM)
    sem = pltpu.SemaphoreType.DMA
    v = pltpu.VMEM
    ig, gwin, gwout = pl.pallas_call(
        kernel,
        name="block_backward",
        out_shape=(
            jax.ShapeDtypeStruct((48, 3072), BF16),
            jax.ShapeDtypeStruct((384, 1536), BF16),
            jax.ShapeDtypeStruct((1024, 384), BF16),
        ),
        in_specs=[hbm, vmem, hbm, hbm, hbm, hbm, hbm],
        out_specs=(hbm, hbm, hbm),
        scratch_shapes=[
            v((4, 768, 768), BF16), v((4, 768, 768), BF16), v((768, 768), BF16),
            v((768, 768), BF16), v((768, 768), F32), v((6, 256, 256), F32),
            v((768, 256), BF16), v((1024, 768), BF16), v((768, 256), BF16),
            v((768, 1536), BF16), v((1536, 1536), BF16), v((8, 1024, 384), BF16),
            v((8, 384, 1536), BF16),
            v((NSO, 6, 2, HO, 384), BF16), v((NSI, 6, 2, HI, 1536), BF16),
            v((1024, 384), BF16), v((384, 1536), BF16), v((4, 384, 768), BF16),
            v((3, 4, 96, 768), BF16), v((4, 48, 768), BF16), v((4, 48, 768), BF16),
            v((48, 3072), F32), v((48, 3072), F32), v((48, 3072), BF16),
            v((48, 3072), BF16), v((48, 128), F32),
            sem((16,)), sem((2, 4, 15)), sem((2, 4, 15)),
            sem((NSO, 6)), sem((NSO, 6)), sem((NSI, 6)), sem((NSI, 6)),
            sem((NSO, 2)), sem((NSO, 2)), sem((NSI, 2)), sem((NSI, 2)),
            sem((4,)), sem((4,)), sem((3, 4)), sem((3, 4)), sem((4,)), sem((4,)),
        ],
        compiler_params=pltpu.CompilerParams(
            collective_id=0, has_side_effects=True, vmem_limit_bytes=63 << 20
        ),
    )(
        block_input_tokens, norm_gain_vector.reshape(1, -1), w_in, w_out, saved_qkv, mlp_pre,
        output_gradient,
    )
    return ig, gwin.astype(F32), gwout.astype(F32)


def solution(mesh):
    placed = (
        P(("dp", "mp"), None),
        P(),
        P(None, "mp"),
        P("mp", None),
        P("dp", "mp"),
        P("dp", "mp"),
        P(("dp", "mp"), None),
    )
    return jax.shard_map(
        body,
        mesh=mesh,
        in_specs=placed,
        out_specs=(P(("dp", "mp"), None), P("dp", "mp"), P("mp", "dp")),
        check_vma=False,
    )
```

```python
import functools

import jax
import jax.numpy as jnp
from jax import lax
from jax.experimental import pallas as pl
from jax.experimental.pallas import tpu as pltpu
from jax.sharding import PartitionSpec as P

HD = 128
F32 = jnp.float32
BF16 = jnp.bfloat16
SCALE = HD ** (-0.5)
MESH = pl.DeviceIdType.MESH
NSO, HO, XO = 2, 128, 512
NSI, HI, XI = 3, 48, 96


def nt(a, b):
    return lax.dot_general(a, b, (((1,), (1,)), ((), ())), preferred_element_type=F32)


def nn(a, b):
    return lax.dot_general(a, b, (((1,), (0,)), ((), ())), preferred_element_type=F32)


def tn(a, b):
    return lax.dot_general(a, b, (((0,), (0,)), ((), ())), preferred_element_type=F32)


def loop(n, fn):
    def step(i, carry):
        fn(i)
        return carry

    lax.fori_loop(0, n, step, 0)


def al(v, m):
    return pl.multiple_of(v, m)


def kernel(
    tok, gain, win, wout, qkv_hbm, pre_hbm, dout,
    ig, gwin, gwout,
    buf_a, buf_b, qkv, pre, slope, pf, heads, joined_t, gh, gproj, wslot, cout, cin,
    rzo, rzi, rfo, rfi, x1o, x1i, rxo, rxi, rs_sib, rs_y, rs_x, ss_x, xhat, gn, own_tok, own_dout, rstd_ref,
    lsem, ag_s, ag_r, zo_s, zo_r, zi_s, zi_r, fo_s, fo_r, fi_s, fi_r, xo_s, xo_r, xi_s, xi_r,
    x1o_s, x1o_r, x1i_s, x1i_r, ms_s, ms_r, my_s, my_r, mx_s, mx_r,
):
    dp = lax.axis_index("dp")
    mp = lax.axis_index("mp")
    z = dp // 2
    xh = dp % 2
    y = mp // 4
    xl = (mp // 2) % 2
    c = mp % 2
    zp, zm, z2 = (z + 1) % 4, (z + 3) % 4, (z + 2) % 4
    yp, ym, y2 = (y + 1) % 4, (y + 3) % 4, (y + 2) % 4
    xn, cn, xo = 1 - xl, 1 - c, 1 - xh

    def m_of(yy, xx, cc):
        return yy * 4 + xx * 2 + cc

    d_sib = (dp, m_of(y, xl, cn))
    d_xn = (dp, m_of(y, xn, c))
    d_yp = (dp, m_of(yp, xl, c))
    d_ym = (dp, m_of(ym, xl, c))
    d_y2 = (dp, m_of(y2, xl, c))
    d_zp = (zp * 2 + xh, mp)
    d_zm = (zm * 2 + xh, mp)
    d_xo = (z * 2 + xo, mp)
    friends = (d_sib, d_xn, d_yp, d_ym, d_y2, d_zp, d_zm, d_xo)

    def load(src, dst, i):
        return pltpu.make_async_copy(src, dst, lsem.at[i])

    l_dout = load(dout, own_dout, 0)
    l_tok = load(tok, own_tok, 1)
    l_qkv = load(qkv_hbm, qkv, 2)
    l_pre = load(pre_hbm, pre, 3)
    for l in (l_dout, l_tok, l_qkv, l_pre):
        l.start()

    def wout_loads(nb, row):
        return [
            load(
                wout.at[pl.ds(nb * 256, 256), pl.ds(h * 1536, 1536)],
                wslot.at[pl.ds(row + h * 256, 256)],
                4 + nb * 2 + h,
            )
            for h in range(2)
        ]

    wo_rows = (0, 512, 1024, 0)
    wo_loads = [wout_loads(nb, wo_rows[nb]) for nb in range(4)]
    for nb in range(3):
        for l in wo_loads[nb]:
            l.start()

    barrier = pltpu.get_barrier_semaphore()
    for d in friends:
        pl.semaphore_signal(barrier, inc=1, device_id=d, device_id_type=MESH)
    pl.semaphore_wait(barrier, len(friends))

    def remote(src, dst, s, r, d):
        return pltpu.make_async_remote_copy(
            src_ref=src, dst_ref=dst, send_sem=s, recv_sem=r, device_id=d, device_id_type=MESH
        )

    order = (z2, zp, zm, z)
    me = m_of(y, xl, c)
    mx = m_of(y, xn, c)
    b_ym, b_yp, b_y2 = m_of(ym, xl, c), m_of(yp, xl, c), m_of(y2, xl, c)
    b_xym, b_xyp, b_xy2 = m_of(ym, xn, c), m_of(yp, xn, c), m_of(y2, xn, c)
    ag_out = (
        (me, 0, d_sib), (me, 0, d_xn), (me, 0, d_yp), (me, 0, d_ym),
        (mx, 0, d_yp), (mx, 0, d_ym), (mx, 0, d_sib),
        (b_ym, 1, d_yp), (b_yp, 2, d_ym), (b_ym, 0, d_sib), (b_yp, 0, d_sib),
        (b_xym, 1, d_yp), (b_xyp, 2, d_ym), (b_xym, 0, d_sib), (b_xyp, 0, d_sib),
        (b_y2, 0, d_sib), (b_xy2, 0, d_sib),
    )
    ag_in = (
        m_of(y, xl, cn), mx, b_ym, b_yp, b_xym, b_xyp, m_of(y, xn, cn),
        b_y2, b_y2, m_of(ym, xl, cn), m_of(yp, xl, cn),
        b_xy2, b_xy2, m_of(ym, xn, cn), m_of(yp, xn, cn), m_of(y2, xl, cn), m_of(y2, xn, cn),
    )
    bufs = (buf_a, buf_b)

    def block(w, o, m, part):
        cols = (slice(None), pl.ds(0, 384), pl.ds(384, 384))[part]
        return bufs[w].at[order[o], pl.ds(al(m * 48, 16), 48), cols]

    def ag_copy(w, o, t, m):
        b = block(w, o, m, ag_out[t][1])
        return remote(b, b, ag_s.at[w, o, t], ag_r.at[w, o, t], ag_out[t][2])

    def ag_send(w, o, ts):
        for t in ts:
            ag_copy(w, o, t, ag_out[t][0]).start()

    def ag_wait(w, o, ts):
        for t in ts:
            ag_copy(w, o, t, ag_in[t]).wait_recv()

    def ag_sx(w, o):
        ag_send(w, o, (1,))

    def ag_sy(w, o):
        ag_send(w, o, (2, 3, 0))

    def ag_x(w, o):
        ag_wait(w, o, (1,))
        ag_send(w, o, (4, 5, 6))

    def ag_y(w, o):
        ag_wait(w, o, (2, 3))
        ag_send(w, o, (7, 8, 9, 10))

    def ag_yx(w, o):
        ag_wait(w, o, (4, 5))
        ag_send(w, o, (11, 12, 13, 14))

    def ag_far(w, o):
        ag_wait(w, o, (7, 8))
        ag_send(w, o, (15,))
        ag_wait(w, o, (11, 12))
        ag_send(w, o, (16,))

    def ag_sib(w, o):
        ag_wait(w, o, (0, 6, 9, 10, 13, 14, 15, 16))

    def ag_drain(w):
        for o in range(4):
            for t in range(17):
                ag_copy(w, o, t, ag_out[t][0]).wait_send()

    l_dout.wait()
    for o in range(4):
        buf_a[order[o], pl.ds(al(me * 48, 16), 48), :] = own_dout[
            :, pl.ds(al(order[o] * 768, 128), 768)
        ]
        ag_sx(0, o)
        if o < 2:
            ag_sy(0, o)

    l_tok.wait()
    x = own_tok[...].astype(F32)
    center = jnp.mean(x, axis=-1, keepdims=True)
    spread = jnp.mean((x - center) ** 2, axis=-1, keepdims=True)
    rstd = 1.0 / jnp.sqrt(spread + 1e-06)
    xhat[...] = (x - center) * rstd
    rstd_ref[...] = jnp.broadcast_to(rstd, rstd_ref.shape)
    for o in range(4):
        buf_b[o, pl.ds(al(me * 48, 16), 48), :] = (
            xhat[:, pl.ds(o * 768, 768)] * gain[:, pl.ds(o * 768, 768)]
        ).astype(BF16)

    for o in range(4):
        ag_sx(1, o)

    def att_fwd(b):
        rows = pl.ds(b * 256, 256)
        for h in range(2):
            q = qkv[rows, pl.ds(h * 128, 128)]
            k = qkv[rows, pl.ds(256 + h * 128, 128)]
            v = qkv[rows, pl.ds(512 + h * 128, 128)]
            s = nt(q, k) * SCALE
            e = jnp.exp(s - jnp.max(s, axis=-1, keepdims=True))
            p = e / jnp.sum(e, axis=-1, keepdims=True)
            pf[b * 2 + h] = p
            out = nn(p.astype(BF16), v)
            heads[rows, pl.ds(h * 128, 128)] = out.astype(BF16)
            joined_t[pl.ds(h * 128, 128), rows] = jnp.transpose(out).astype(BF16)

    def gelu(t):
        rows = pl.ds(al(t * 128, 128), 128)
        v = pre[rows, :].astype(F32)
        cumul = 0.5 * (1.0 + lax.erf(v * 0.7071067811865476))
        joined_t[pl.ds(256, 768), rows] = jnp.transpose(v * cumul).astype(BF16)
        dens = jnp.exp(-0.5 * v * v) * 0.3989422804014327
        slope[rows, :] = cumul + v * dens

    l_qkv.wait()
    att_fwd(0)
    ag_x(0, 0)
    att_fwd(1)
    ag_y(0, 0)
    ag_sy(0, 2)
    ag_x(0, 1)
    att_fwd(2)
    ag_yx(0, 0)
    ag_y(0, 1)
    ag_sy(0, 3)
    ag_x(0, 2)
    l_pre.wait()
    gelu(0)
    gelu(1)
    ag_far(0, 0)
    ag_yx(0, 1)
    ag_x(0, 3)
    gelu(2)
    gelu(3)
    ag_y(0, 2)
    gelu(4)
    gelu(5)
    ag_sib(0, 0)

    class Ring:
        def __init__(self, src, rbuf, ssem, rsem, add):
            self.src, self.rbuf, self.ssem, self.rsem, self.add = src, rbuf, ssem, rsem, add
            self.sent = []

        def send(self, i, src, d):
            cp = remote(src, self.rbuf.at[i], self.ssem.at[i], self.rsem.at[i], d)
            cp.start()
            self.sent.append(cp)

        def wait(self, i):
            b = self.rbuf.at[i]
            remote(b, b, self.ssem.at[i], self.rsem.at[i], d_zp).wait_recv()

        def far(self):
            self.send(0, self.src(z2, 1), d_zp)
            self.send(1, self.src(z2, 0), d_zm)

        def near_p(self):
            self.send(2, self.src(zp, 0), d_zp)

        def near_m(self):
            self.send(3, self.src(zm, 1), d_zm)

        def relay_p(self):
            self.wait(0)
            self.add(self.rbuf.at[0], self.src(zp, 1))
            self.send(4, self.rbuf.at[0], d_zp)

        def relay_m(self):
            self.wait(1)
            self.add(self.rbuf.at[1], self.src(zm, 0))
            self.send(5, self.rbuf.at[1], d_zm)

        def arrived(self):
            for i in (2, 3, 4, 5):
                self.wait(i)

        def drain(self):
            for cp in self.sent:
                cp.wait_send()

    def adder(lead, height, tile):
        def add(dst, src):
            def step(i):
                rows = pl.ds(al(i * tile, tile), tile)
                for at in lead:
                    dst[at + (rows, slice(None))] = (
                        dst[at + (rows, slice(None))].astype(F32)
                        + src[at + (rows, slice(None))].astype(F32)
                    ).astype(BF16)

            loop(height // tile, step)

        return add

    def z_first(part, base, height):
        return lambda zz, half: part.at[pl.ds(zz * 2, 2), pl.ds(base + half * height, height), :]

    def x_first(part, base, height):
        return lambda zz, half: part.at[zz * 2 + xh, pl.ds(base + half * height, height), :]

    both = ((0,), (1,))
    ro = [
        Ring(z_first(cout, s * 2 * HO, HO), rzo.at[s], zo_s.at[s], zo_r.at[s], adder(both, HO, 64))
        for s in range(NSO)
    ]
    ri = [
        Ring(z_first(cin, s * 2 * HI, HI), rzi.at[s], zi_s.at[s], zi_r.at[s], adder(both, HI, 16))
        for s in range(NSI)
    ]
    base_o, base_i = 1024 - XO, 384 - XI
    fo = Ring(x_first(cout, base_o, XO // 2), rfo, fo_s, fo_r, adder(((),), XO // 2, 64))
    fi = Ring(x_first(cin, base_i, XI // 2), rfi, fi_s, fi_r, adder(((),), XI // 2, 16))

    class Cross:
        def __init__(self, ring, part, rx, ssem, rsem, base, height, tile):
            self.ring, self.part, self.rx = ring, part, rx
            self.ssem, self.rsem = ssem, rsem
            self.base, self.height, self.tile = base, height, tile
            self.sent = []

        def send(self):
            self.ring.arrived()
            r = self.ring.rbuf
            for half, (a, b) in enumerate(((2, 5), (3, 4))):
                off = self.base + half * self.height

                def step(i, a=a, b=b, off=off):
                    rows = pl.ds(al(i * self.tile, self.tile), self.tile)
                    prow = pl.ds(al(off + i * self.tile, self.tile), self.tile)
                    r[a, xo, rows, :] = (
                        r[a, xo, rows, :].astype(F32)
                        + r[b, xo, rows, :].astype(F32)
                        + self.part[z * 2 + xo, prow, :].astype(F32)
                    ).astype(BF16)

                loop(self.height // self.tile, step)
                cp = remote(
                    r.at[a, xo], self.rx.at[pl.ds(off, self.height), :],
                    self.ssem.at[half], self.rsem.at[half], d_xo,
                )
                cp.start()
                self.sent.append(cp)

        def finish(self):
            r = self.ring.rbuf
            for half, (a, b) in enumerate(((2, 5), (3, 4))):
                off = self.base + half * self.height
                dst = self.rx.at[pl.ds(off, self.height), :]
                remote(dst, dst, self.ssem.at[half], self.rsem.at[half], d_xo).wait_recv()

                def step(i, a=a, b=b, off=off):
                    rows = pl.ds(al(i * self.tile, self.tile), self.tile)
                    prow = pl.ds(al(off + i * self.tile, self.tile), self.tile)
                    self.rx[prow, :] = (
                        r[a, xh, rows, :].astype(F32)
                        + r[b, xh, rows, :].astype(F32)
                        + self.part[z * 2 + xh, prow, :].astype(F32)
                        + self.rx[prow, :].astype(F32)
                    ).astype(BF16)

                loop(self.height // self.tile, step)

        def drain(self):
            for cp in self.sent:
                cp.wait_send()

    class First:
        def __init__(self, ring, part, x1, rx, ssem, rsem, base, height, tile):
            self.ring, self.part, self.x1, self.rx = ring, part, x1, rx
            self.ssem, self.rsem = ssem, rsem
            self.base, self.height, self.tile = base, height, tile

        def copy(self, o):
            return remote(
                self.part.at[order[o] * 2 + xo, pl.ds(self.base, self.height), :],
                self.x1.at[o], self.ssem.at[o], self.rsem.at[o], d_xo,
            )

        def send(self, o):
            self.copy(o).start()

        def take(self, o):
            self.copy(o).wait_recv()

            def step(i):
                rows = pl.ds(al(i * self.tile, self.tile), self.tile)
                prow = pl.ds(al(self.base + i * self.tile, self.tile), self.tile)
                mine = order[o] * 2 + xh
                self.part[mine, prow, :] = (
                    self.part[mine, prow, :].astype(F32) + self.x1[o, rows, :].astype(F32)
                ).astype(BF16)

            loop(self.height // self.tile, step)
            if o < 3:
                (self.ring.far, self.ring.near_p, self.ring.near_m)[o]()

        def finish(self):
            self.ring.arrived()
            r = self.ring.rbuf
            half_rows = self.height // 2
            for half, (a, b) in enumerate(((2, 5), (3, 4))):
                off = self.base + half * half_rows

                def step(i, a=a, b=b, off=off):
                    rows = pl.ds(al(i * self.tile, self.tile), self.tile)
                    prow = pl.ds(al(off + i * self.tile, self.tile), self.tile)
                    self.rx[prow, :] = (
                        r[a, rows, :].astype(F32)
                        + r[b, rows, :].astype(F32)
                        + self.part[z * 2 + xh, prow, :].astype(F32)
                    ).astype(BF16)

                loop(half_rows // self.tile, step)

        def drain(self):
            for o in range(4):
                self.copy(o).wait_send()

    co = [
        Cross(ro[s], cout, rxo, xo_s.at[s], xo_r.at[s], s * 2 * HO, HO, 64) for s in range(NSO)
    ]
    ci = [
        Cross(ri[s], cin, rxi, xi_s.at[s], xi_r.at[s], s * 2 * HI, HI, 16) for s in range(NSI)
    ]
    xfo = First(fo, cout, x1o, rxo, x1o_s, x1o_r, base_o, XO, 64)
    xfi = First(fi, cin, x1i, rxi, x1i_s, x1i_r, base_i, XI, 16)

    def out_chunk(o):
        j = order[o]

        def step(r):
            rows = pl.ds(al(r * 256, 256), 256)
            t = nn(joined_t[rows, :], buf_a[j]).astype(BF16)
            cout[j * 2, rows, :] = t[:, :384]
            cout[j * 2 + 1, rows, :] = t[:, 384:]

        loop(4, step)

    out_chunk(0)
    for r in ro:
        r.far()
    xfo.send(0)
    ag_far(0, 1)
    ag_yx(0, 2)
    ag_y(0, 3)
    ag_sy(1, 0)
    ag_sib(0, 1)
    out_chunk(1)
    for r in ro:
        r.near_p()
    xfo.send(1)
    ag_far(0, 2)
    ag_yx(0, 3)
    ag_x(1, 0)
    ag_sy(1, 1)
    ag_sib(0, 2)
    out_chunk(2)
    for r in ro:
        r.near_m()
    xfo.send(2)
    ag_far(0, 3)
    ag_x(1, 1)
    ag_y(1, 0)
    ag_sy(1, 2)
    ag_sib(0, 3)
    out_chunk(3)
    xfo.send(3)
    ag_yx(1, 0)
    ag_y(1, 1)
    ag_x(1, 2)
    ag_sy(1, 3)
    ag_x(1, 3)

    def joined_grad(nb):
        for l in wo_loads[nb]:
            l.wait()
        row = wo_rows[nb]

        def step(r):
            rows = pl.ds(al(r * 384, 128), 384)
            acc = jnp.zeros((384, 256), F32)
            for j in range(4):
                w = wslot[pl.ds(row + (j // 2) * 256, 256), pl.ds((j % 2) * 768, 768)]
                acc = acc + nt(buf_a[j, rows, :], w)
            g = acc.astype(BF16)
            if nb == 0:
                gh[rows, :] = g
            else:
                cols = pl.ds((nb - 1) * 256, 256)
                gproj[rows, pl.ds(768 + (nb - 1) * 256, 256)] = (
                    g.astype(F32) * slope[rows, cols]
                ).astype(BF16)

        loop(2, step)

    joined_grad(0)
    for l in wo_loads[3]:
        l.start()
    ag_far(1, 0)
    ag_yx(1, 1)
    ro[0].relay_p()
    ro[0].relay_m()
    joined_grad(1)
    ag_y(1, 2)
    xfo.take(0)
    joined_grad(2)
    ag_far(1, 1)
    ag_yx(1, 2)
    ro[1].relay_p()
    ro[1].relay_m()
    joined_grad(3)
    ag_y(1, 3)

    def win_load(j):
        return load(
            win.at[pl.ds(j * 768, 768), :], wslot.at[pl.ds((j % 2) * 768, 768)], 12 + j
        )

    win_load(0).start()
    win_load(1).start()

    def att_bwd(b):
        rows = pl.ds(b * 256, 256)
        for h in range(2):
            q = qkv[rows, pl.ds(h * 128, 128)]
            k = qkv[rows, pl.ds(256 + h * 128, 128)]
            v = qkv[rows, pl.ds(512 + h * 128, 128)]
            g = gh[rows, pl.ds(h * 128, 128)]
            p = pf[b * 2 + h]
            delta = jnp.sum(
                g.astype(F32) * heads[rows, pl.ds(h * 128, 128)].astype(F32),
                axis=-1, keepdims=True,
            )
            ds = (p * (nt(g, v) - delta) * SCALE).astype(BF16)
            gproj[rows, pl.ds(512 + h * 128, 128)] = tn(p.astype(BF16), g).astype(BF16)
            gproj[rows, pl.ds(h * 128, 128)] = nn(ds, k).astype(BF16)
            gproj[rows, pl.ds(256 + h * 128, 128)] = tn(ds, q).astype(BF16)

    att_bwd(0)
    ag_far(1, 2)
    ag_yx(1, 3)
    att_bwd(1)
    xfo.take(1)
    att_bwd(2)
    ag_far(1, 3)

    ag_drain(0)

    def transposed(o):
        ag_sib(1, o)
        j = order[o]

        def step(i):
            rows = pl.ds(al(i * 128, 128), 128)
            buf_a[j, :, rows] = jnp.transpose(buf_b[j, rows, :])

        loop(6, step)

    def in_chunk(o):
        j = order[o]

        def step(i):
            h, n = i // 2, i % 2
            rows = pl.ds(al(h * 384, 128), 384)
            cols = pl.ds(al(n * 768, 128), 768)
            cin[j * 2 + h, :, cols] = nn(buf_a[j, rows, :], gproj[:, cols]).astype(BF16)

        loop(4, step)

    transposed(0)
    in_chunk(0)
    for r in ri:
        r.far()
    xfi.send(0)
    transposed(1)
    in_chunk(1)
    for r in ri:
        r.near_p()
    xfi.send(1)
    xfo.take(2)
    transposed(2)
    in_chunk(2)
    for r in ri:
        r.near_m()
    xfi.send(2)
    transposed(3)
    in_chunk(3)
    xfi.send(3)
    xfo.take(3)
    fo.relay_p()
    fo.relay_m()
    ag_drain(1)

    def sib_copy(j):
        return remote(
            buf_b.at[j, pl.ds(al(cn * 384, 128), 384), :], rs_sib.at[j],
            ms_s.at[j], ms_r.at[j], d_sib,
        )

    def normed_grad(j):
        win_load(j).wait()
        base = (j % 2) * 768

        def step(i):
            h, n = i // 3, i % 3
            rows = pl.ds(al(h * 384, 128), 384)
            w = wslot[pl.ds(al(base + n * 256, 256), 256), :]
            t = nt(gproj[rows, :], w).astype(BF16)
            cols = pl.ds(al(n * 256, 128), 256)
            for b in range(8):
                buf_b[j, pl.ds(al((b % 2) * 384 + (h * 4 + b // 2) * 48, 16), 48), cols] = t[
                    b * 48 : b * 48 + 48
                ]

        loop(6, step)
        sib_copy(j).start()
        if j < 2:
            win_load(j + 2).start()

    y_rows = {0: yp, 1: ym, 2: y2}
    y_dev = (d_yp, d_ym, d_y2)

    def y_copy(j, i):
        return remote(
            buf_b.at[j, pl.ds(al(c * 384 + y_rows[i] * 96, 16), 96), :], rs_y.at[i, j],
            my_s.at[i, j], my_r.at[i, j], y_dev[i],
        )

    def sib_sum(j):
        sib_copy(j).wait_recv()

        def step(i):
            rows = pl.ds(al(c * 384 + i * 48, 16), 48)
            buf_b[j, rows, :] = (
                buf_b[j, rows, :].astype(F32)
                + rs_sib[j, pl.ds(al(i * 48, 16), 48), :].astype(F32)
            ).astype(BF16)

        loop(8, step)
        for i in range(3):
            y_copy(j, i).start()

    def x_copy(j):
        return remote(ss_x.at[j], rs_x.at[j], mx_s.at[j], mx_r.at[j], d_xn)

    def y_sum(j):
        for i in range(3):
            y_copy(j, i).wait_recv()

        def total(side):
            acc = buf_b[j, pl.ds(al(c * 384 + y * 96 + side * 48, 16), 48), :].astype(F32)
            for i in range(3):
                acc = acc + rs_y[i, j, pl.ds(al(side * 48, 16), 48), :].astype(F32)
            return acc

        ss_x[j] = total(xn).astype(BF16)
        x_copy(j).start()
        gn[:, pl.ds(j * 768, 768)] = total(xl)

    def x_sum(j):
        x_copy(j).wait_recv()
        cols = pl.ds(j * 768, 768)
        gn[:, cols] = gn[:, cols] + rs_x[j].astype(F32)

    normed_grad(0)
    ri[0].relay_p()
    ri[0].relay_m()
    normed_grad(1)
    sib_sum(0)
    normed_grad(2)
    sib_sum(1)
    ri[1].relay_p()
    ri[1].relay_m()
    normed_grad(3)
    sib_sum(2)
    co[0].send()
    co[1].send()
    sib_sum(3)
    xfi.take(0)
    ri[2].relay_p()
    ri[2].relay_m()
    y_sum(0)
    y_sum(1)
    xfi.take(1)
    xfo.finish()
    y_sum(2)
    y_sum(3)
    xfi.take(2)
    co[0].finish()
    co[1].finish()
    st_o = load(rxo, gwout, 0)
    st_o.start()
    xfi.take(3)
    for j in range(4):
        x_sum(j)
    xh_v = xhat[...]
    sg = gn[...] * gain[...]
    m1 = jnp.mean(sg, axis=-1, keepdims=True)
    m2 = jnp.mean(sg * xh_v, axis=-1, keepdims=True)
    own_tok[...] = (
        own_dout[...].astype(F32) + (sg - m1 - xh_v * m2) * rstd_ref[:, :1]
    ).astype(BF16)
    st_g = load(own_tok, ig, 1)
    st_g.start()
    ci[0].send()
    fi.relay_p()
    fi.relay_m()
    ci[1].send()
    ci[2].send()
    for s in range(NSI):
        ci[s].finish()
    xfi.finish()
    st_i = load(rxi, gwin, 2)
    st_i.start()
    for r in ro + ri + [fo, fi] + co + ci + [xfo, xfi]:
        r.drain()
    for j in range(4):
        sib_copy(j).wait_send()
        x_copy(j).wait_send()
        for i in range(3):
            y_copy(j, i).wait_send()
    st_o.wait()
    st_g.wait()
    st_i.wait()


def body(block_input_tokens, norm_gain_vector, w_in, w_out, saved_qkv, mlp_pre, output_gradient):
    hbm = pl.BlockSpec(memory_space=pl.ANY)
    vmem = pl.BlockSpec(memory_space=pltpu.VMEM)
    sem = pltpu.SemaphoreType.DMA
    v = pltpu.VMEM
    ig, gwin, gwout = pl.pallas_call(
        kernel,
        name="block_backward",
        out_shape=(
            jax.ShapeDtypeStruct((48, 3072), BF16),
            jax.ShapeDtypeStruct((384, 1536), BF16),
            jax.ShapeDtypeStruct((1024, 384), BF16),
        ),
        in_specs=[hbm, vmem, hbm, hbm, hbm, hbm, hbm],
        out_specs=(hbm, hbm, hbm),
        scratch_shapes=[
            v((4, 768, 768), BF16), v((4, 768, 768), BF16), v((768, 768), BF16),
            v((768, 768), BF16), v((768, 768), F32), v((6, 256, 256), F32),
            v((768, 256), BF16), v((1024, 768), BF16), v((768, 256), BF16),
            v((768, 1536), BF16), v((1536, 1536), BF16), v((8, 1024, 384), BF16),
            v((8, 384, 1536), BF16),
            v((NSO, 6, 2, HO, 384), BF16), v((NSI, 6, 2, HI, 1536), BF16),
            v((6, XO // 2, 384), BF16), v((6, XI // 2, 1536), BF16),
            v((4, XO, 384), BF16), v((4, XI, 1536), BF16),
            v((1024, 384), BF16), v((384, 1536), BF16), v((4, 384, 768), BF16),
            v((3, 4, 96, 768), BF16), v((4, 48, 768), BF16), v((4, 48, 768), BF16),
            v((48, 3072), F32), v((48, 3072), F32), v((48, 3072), BF16),
            v((48, 3072), BF16), v((48, 128), F32),
            sem((16,)), sem((2, 4, 17)), sem((2, 4, 17)),
            sem((NSO, 6)), sem((NSO, 6)), sem((NSI, 6)), sem((NSI, 6)),
            sem((6,)), sem((6,)), sem((6,)), sem((6,)),
            sem((NSO, 2)), sem((NSO, 2)), sem((NSI, 2)), sem((NSI, 2)),
            sem((4,)), sem((4,)), sem((4,)), sem((4,)),
            sem((4,)), sem((4,)), sem((3, 4)), sem((3, 4)), sem((4,)), sem((4,)),
        ],
        compiler_params=pltpu.CompilerParams(
            collective_id=0, has_side_effects=True, vmem_limit_bytes=63 << 20
        ),
    )(
        block_input_tokens, norm_gain_vector.reshape(1, -1), w_in, w_out, saved_qkv, mlp_pre,
        output_gradient,
    )
    return ig, gwin.astype(F32), gwout.astype(F32)


def solution(mesh):
    placed = (
        P(("dp", "mp"), None),
        P(),
        P(None, "mp"),
        P("mp", None),
        P("dp", "mp"),
        P("dp", "mp"),
        P(("dp", "mp"), None),
    )
    return jax.shard_map(
        body,
        mesh=mesh,
        in_specs=placed,
        out_specs=(P(("dp", "mp"), None), P("dp", "mp"), P("mp", "dp")),
        check_vma=False,
    )
```

```python
import functools

import jax
import jax.numpy as jnp
from jax import lax
from jax.experimental import pallas as pl
from jax.experimental.pallas import tpu as pltpu
from jax.sharding import PartitionSpec as P

HD = 128
F32 = jnp.float32
BF16 = jnp.bfloat16
SCALE = HD ** (-0.5)
MESH = pl.DeviceIdType.MESH
NSO, HO, XO = 2, 128, 512
NSI, HI, XI = 3, 48, 96


def nt(a, b):
    return lax.dot_general(a, b, (((1,), (1,)), ((), ())), preferred_element_type=F32)


def nn(a, b):
    return lax.dot_general(a, b, (((1,), (0,)), ((), ())), preferred_element_type=F32)


def tn(a, b):
    return lax.dot_general(a, b, (((0,), (0,)), ((), ())), preferred_element_type=F32)


def loop(n, fn):
    def step(i, carry):
        fn(i)
        return carry

    lax.fori_loop(0, n, step, 0)


def al(v, m):
    return pl.multiple_of(v, m)


def kernel(
    tok, gain, win, wout, qkv_hbm, pre_hbm, dout,
    ig, gwin, gwout,
    buf_a, buf_b, qkv, pre, slope, pf, heads, joined_t, gh, gproj, wslot, cout, cin,
    rzo, rzi, rfo, rfi, x1o, x1i, rxo, rxi, rs_sib, rs_y, rs_x, ss_x, xhat, gn,
    own_tok, own_dout, rstd_ref,
    lsem, ag_s, ag_r, zo_s, zo_r, zi_s, zi_r, fo_s, fo_r, fi_s, fi_r, xo_s, xo_r, xi_s, xi_r,
    x1o_s, x1o_r, x1i_s, x1i_r, m_s, ms_r, my_r, mx_r,
):
    dp = lax.axis_index("dp")
    mp = lax.axis_index("mp")
    z = dp // 2
    xh = dp % 2
    y = mp // 4
    xl = (mp // 2) % 2
    c = mp % 2
    zp, zm, z2 = (z + 1) % 4, (z + 3) % 4, (z + 2) % 4
    yp, ym, y2 = (y + 1) % 4, (y + 3) % 4, (y + 2) % 4
    xn, cn, xo = 1 - xl, 1 - c, 1 - xh

    def m_of(yy, xx, cc):
        return yy * 4 + xx * 2 + cc

    d_sib = (dp, m_of(y, xl, cn))
    d_xn = (dp, m_of(y, xn, c))
    d_yp = (dp, m_of(yp, xl, c))
    d_ym = (dp, m_of(ym, xl, c))
    d_y2 = (dp, m_of(y2, xl, c))
    d_zp = (zp * 2 + xh, mp)
    d_zm = (zm * 2 + xh, mp)
    d_xo = (z * 2 + xo, mp)
    friends = (d_sib, d_xn, d_yp, d_ym, d_y2, d_zp, d_zm, d_xo)

    def load(src, dst, i):
        return pltpu.make_async_copy(src, dst, lsem.at[i])

    own = 2 * y + xl
    order = (z2, zp, zm, z)
    l_dout = load(dout, own_dout, 12)
    l_tok = load(tok, own_tok, 0)
    l_qkv = load(qkv_hbm, qkv, 2)
    l_pre = load(pre_hbm, pre, 3)
    for l in (l_dout, l_tok, l_qkv, l_pre):
        l.start()

    def wout_loads(nb, row):
        return [
            load(
                wout.at[pl.ds(nb * 256, 256), pl.ds(h * 1536, 1536)],
                wslot.at[pl.ds(row + h * 256, 256)],
                4 + nb * 2 + h,
            )
            for h in range(2)
        ]

    wo_rows = (0, 512, 1024, 0)
    wo_loads = [wout_loads(nb, wo_rows[nb]) for nb in range(4)]
    for nb in range(3):
        for l in wo_loads[nb]:
            l.start()

    barrier = pltpu.get_barrier_semaphore()
    for d in friends:
        pl.semaphore_signal(barrier, inc=1, device_id=d, device_id_type=MESH)
    pl.semaphore_wait(barrier, len(friends))

    def remote(src, dst, s, r, d):
        return pltpu.make_async_remote_copy(
            src_ref=src, dst_ref=dst, send_sem=s, recv_sem=r, device_id=d, device_id_type=MESH
        )

    bufs = (buf_a, buf_b)
    pair, pair_p, pair_m, pair_2 = (pl.ds(2 * v, 2) for v in (y, yp, ym, y2))
    whole, left, right = slice(None), pl.ds(0, 384), pl.ds(384, 384)

    def ag_copy(w, o, kind, at, core, cols, d):
        b = bufs[w].at[order[o], at, core, :, cols]
        sent = ag_s.at[w, 0 if kind == 0 else 1]
        return remote(b, b, sent, ag_r.at[w, o, kind], d)

    def ag_wait(w, o, kind, at, core):
        ag_copy(w, o, kind, at, core, whole, d_sib).wait_recv()

    def ag_sx(w, o):
        ag_copy(w, o, 0, own, c, whole, d_xn).start()

    def ag_sy(w, o):
        ag_copy(w, o, 1, own, c, whole, d_yp).start()
        ag_copy(w, o, 1, own, c, whole, d_ym).start()

    def ag_x(w, o):
        ag_wait(w, o, 0, 2 * y + xn, c)
        at = 2 * y + xn if w == 0 and o < 2 else pair
        ag_copy(w, o, 1, at, c, whole, d_yp).start()
        ag_copy(w, o, 1, at, c, whole, d_ym).start()
        ag_copy(w, o, 3, pair, c, whole, d_sib).start()

    def ag_y(w, o):
        ag_wait(w, o, 1, pl.ds(0, 4), c)
        ag_copy(w, o, 2, pair_m, c, left, d_yp).start()
        ag_copy(w, o, 2, pair_p, c, right, d_ym).start()
        ag_copy(w, o, 3, pair_m, c, whole, d_sib).start()
        ag_copy(w, o, 3, pair_p, c, whole, d_sib).start()

    def ag_far(w, o):
        ag_wait(w, o, 2, pair_2, c)
        ag_copy(w, o, 3, pair_2, c, whole, d_sib).start()

    def ag_sib(w, o):
        ag_wait(w, o, 3, whole, cn)

    def ag_drain(w):
        for i, b in enumerate((bufs[w].at[:, own, c], bufs[w].at[:, pl.ds(0, 7)])):
            remote(b, b, ag_s.at[w, i], ag_r.at[w, 0, 0], d_sib).wait_send()

    l_dout.wait()
    for o in range(4):
        buf_a[order[o], own, c] = own_dout[:, pl.ds(al(order[o] * 768, 128), 768)]
        ag_sx(0, o)
        if o < 2:
            ag_sy(0, o)

    l_tok.wait()
    x = own_tok[...].astype(F32)
    center = jnp.mean(x, axis=-1, keepdims=True)
    spread = jnp.mean((x - center) ** 2, axis=-1, keepdims=True)
    rstd = 1.0 / jnp.sqrt(spread + 1e-06)
    xhat[...] = (x - center) * rstd
    rstd_ref[...] = jnp.broadcast_to(rstd, rstd_ref.shape)
    for o in range(4):
        buf_b[o, own, c] = (
            xhat[:, pl.ds(o * 768, 768)] * gain[:, pl.ds(o * 768, 768)]
        ).astype(BF16)

    for o in range(4):
        ag_sx(1, o)

    def att_fwd(b):
        rows = pl.ds(b * 256, 256)
        for h in range(2):
            q = qkv[rows, pl.ds(h * 128, 128)]
            k = qkv[rows, pl.ds(256 + h * 128, 128)]
            v = qkv[rows, pl.ds(512 + h * 128, 128)]
            s = nt(q, k) * SCALE
            e = jnp.exp(s - jnp.max(s, axis=-1, keepdims=True))
            p = e / jnp.sum(e, axis=-1, keepdims=True)
            pf[b * 2 + h] = p
            out = nn(p.astype(BF16), v)
            heads[rows, pl.ds(h * 128, 128)] = out.astype(BF16)
            joined_t[pl.ds(h * 128, 128), rows] = jnp.transpose(out).astype(BF16)

    def gelu(t):
        rows = pl.ds(al(t * 128, 128), 128)
        v = pre[rows, :].astype(F32)
        cumul = 0.5 * (1.0 + lax.erf(v * 0.7071067811865476))
        joined_t[pl.ds(256, 768), rows] = jnp.transpose(v * cumul).astype(BF16)
        dens = jnp.exp(-0.5 * v * v) * 0.3989422804014327
        slope[rows, :] = cumul + v * dens

    l_pre.wait()
    gelu(0)
    ag_x(0, 0)
    l_qkv.wait()
    gelu(1)
    ag_x(0, 1)
    att_fwd(0)
    att_fwd(1)
    att_fwd(2)
    gelu(2)
    ag_y(0, 0)
    ag_x(0, 2)
    gelu(3)
    gelu(4)
    gelu(5)
    ag_y(0, 1)
    ag_x(0, 3)
    ag_far(0, 0)
    ag_sib(0, 0)

    class Ring:
        def __init__(self, src, rbuf, ssem, rsem, add):
            self.src, self.rbuf, self.ssem, self.rsem, self.add = src, rbuf, ssem, rsem, add
            self.sent = []

        def send(self, i, src, d):
            cp = remote(src, self.rbuf.at[i], self.ssem.at[i], self.rsem.at[i], d)
            cp.start()
            self.sent.append(cp)

        def wait(self, i):
            b = self.rbuf.at[i]
            remote(b, b, self.ssem.at[i], self.rsem.at[i], d_zp).wait_recv()

        def far(self):
            self.send(0, self.src(z2, 1), d_zp)
            self.send(1, self.src(z2, 0), d_zm)

        def near_p(self):
            self.send(2, self.src(zp, 0), d_zp)

        def near_m(self):
            self.send(3, self.src(zm, 1), d_zm)

        def relay_p(self):
            self.wait(0)
            self.add(self.rbuf.at[0], self.src(zp, 1))
            self.send(4, self.rbuf.at[0], d_zp)

        def relay_m(self):
            self.wait(1)
            self.add(self.rbuf.at[1], self.src(zm, 0))
            self.send(5, self.rbuf.at[1], d_zm)

        def arrived(self):
            for i in (2, 3, 4, 5):
                self.wait(i)

        def drain(self):
            for cp in self.sent:
                cp.wait_send()

    def adder(lead, height, tile):
        def add(dst, src):
            def step(i):
                rows = pl.ds(al(i * tile, tile), tile)
                for at in lead:
                    dst[at + (rows, slice(None))] = (
                        dst[at + (rows, slice(None))].astype(F32)
                        + src[at + (rows, slice(None))].astype(F32)
                    ).astype(BF16)

            loop(height // tile, step)

        return add

    def z_first(part, base, height):
        return lambda zz, half: part.at[pl.ds(zz * 2, 2), pl.ds(base + half * height, height), :]

    def x_first(part, base, height):
        return lambda zz, half: part.at[zz * 2 + xh, pl.ds(base + half * height, height), :]

    both = ((0,), (1,))
    ro = [
        Ring(z_first(cout, s * 2 * HO, HO), rzo.at[s], zo_s.at[s], zo_r.at[s], adder(both, HO, 64))
        for s in range(NSO)
    ]
    ri = [
        Ring(z_first(cin, s * 2 * HI, HI), rzi.at[s], zi_s.at[s], zi_r.at[s], adder(both, HI, 16))
        for s in range(NSI)
    ]
    base_o, base_i = 1024 - XO, 384 - XI
    fo = Ring(x_first(cout, base_o, XO // 2), rfo, fo_s, fo_r, adder(((),), XO // 2, 64))
    fi = Ring(x_first(cin, base_i, XI // 2), rfi, fi_s, fi_r, adder(((),), XI // 2, 16))

    class Cross:
        def __init__(self, ring, part, rx, ssem, rsem, base, height, tile):
            self.ring, self.part, self.rx = ring, part, rx
            self.ssem, self.rsem = ssem, rsem
            self.base, self.height, self.tile = base, height, tile
            self.sent = []

        def send(self):
            self.ring.arrived()
            r = self.ring.rbuf
            for half, (a, b) in enumerate(((2, 5), (3, 4))):
                off = self.base + half * self.height

                def step(i, a=a, b=b, off=off):
                    rows = pl.ds(al(i * self.tile, self.tile), self.tile)
                    prow = pl.ds(al(off + i * self.tile, self.tile), self.tile)
                    r[a, xo, rows, :] = (
                        r[a, xo, rows, :].astype(F32)
                        + r[b, xo, rows, :].astype(F32)
                        + self.part[z * 2 + xo, prow, :].astype(F32)
                    ).astype(BF16)

                loop(self.height // self.tile, step)
                cp = remote(
                    r.at[a, xo], self.rx.at[pl.ds(off, self.height), :],
                    self.ssem.at[half], self.rsem.at[half], d_xo,
                )
                cp.start()
                self.sent.append(cp)

        def finish(self):
            r = self.ring.rbuf
            for half, (a, b) in enumerate(((2, 5), (3, 4))):
                off = self.base + half * self.height
                dst = self.rx.at[pl.ds(off, self.height), :]
                remote(dst, dst, self.ssem.at[half], self.rsem.at[half], d_xo).wait_recv()

                def step(i, a=a, b=b, off=off):
                    rows = pl.ds(al(i * self.tile, self.tile), self.tile)
                    prow = pl.ds(al(off + i * self.tile, self.tile), self.tile)
                    self.rx[prow, :] = (
                        r[a, xh, rows, :].astype(F32)
                        + r[b, xh, rows, :].astype(F32)
                        + self.part[z * 2 + xh, prow, :].astype(F32)
                        + self.rx[prow, :].astype(F32)
                    ).astype(BF16)

                loop(self.height // self.tile, step)

        def drain(self):
            for cp in self.sent:
                cp.wait_send()

    class First:
        def __init__(self, ring, part, x1, rx, ssem, rsem, base, height, tile):
            self.ring, self.part, self.x1, self.rx = ring, part, x1, rx
            self.ssem, self.rsem = ssem, rsem
            self.base, self.height, self.tile = base, height, tile

        def copy(self, o):
            return remote(
                self.part.at[order[o] * 2 + xo, pl.ds(self.base, self.height), :],
                self.x1.at[o], self.ssem.at[o], self.rsem.at[o], d_xo,
            )

        def send(self, o):
            self.copy(o).start()

        def take(self, o):
            self.copy(o).wait_recv()

            def step(i):
                rows = pl.ds(al(i * self.tile, self.tile), self.tile)
                prow = pl.ds(al(self.base + i * self.tile, self.tile), self.tile)
                mine = order[o] * 2 + xh
                self.part[mine, prow, :] = (
                    self.part[mine, prow, :].astype(F32) + self.x1[o, rows, :].astype(F32)
                ).astype(BF16)

            loop(self.height // self.tile, step)
            if o < 3:
                (self.ring.far, self.ring.near_p, self.ring.near_m)[o]()

        def finish(self):
            self.ring.arrived()
            r = self.ring.rbuf
            half_rows = self.height // 2
            for half, (a, b) in enumerate(((2, 5), (3, 4))):
                off = self.base + half * half_rows

                def step(i, a=a, b=b, off=off):
                    rows = pl.ds(al(i * self.tile, self.tile), self.tile)
                    prow = pl.ds(al(off + i * self.tile, self.tile), self.tile)
                    self.rx[prow, :] = (
                        r[a, rows, :].astype(F32)
                        + r[b, rows, :].astype(F32)
                        + self.part[z * 2 + xh, prow, :].astype(F32)
                    ).astype(BF16)

                loop(half_rows // self.tile, step)

        def drain(self):
            for o in range(4):
                self.copy(o).wait_send()

    co = [
        Cross(ro[s], cout, rxo, xo_s.at[s], xo_r.at[s], s * 2 * HO, HO, 64) for s in range(NSO)
    ]
    ci = [
        Cross(ri[s], cin, rxi, xi_s.at[s], xi_r.at[s], s * 2 * HI, HI, 16) for s in range(NSI)
    ]
    xfo = First(fo, cout, x1o, rxo, x1o_s, x1o_r, base_o, XO, 64)
    xfi = First(fi, cin, x1i, rxi, x1i_s, x1i_r, base_i, XI, 16)

    def out_chunk(o):
        j = order[o]

        def step(r):
            rows = pl.ds(al(r * 256, 256), 256)
            t = nn(joined_t[rows, :], buf_a[j].reshape(768, 768)).astype(BF16)
            cout[j * 2, rows, :] = t[:, :384]
            cout[j * 2 + 1, rows, :] = t[:, 384:]

        loop(4, step)

    out_chunk(0)
    for r in ro:
        r.far()
    xfo.send(0)
    ag_far(0, 1)
    ag_y(0, 2)
    ag_sib(0, 1)
    out_chunk(1)
    for r in ro:
        r.near_p()
    xfo.send(1)
    ag_far(0, 2)
    ag_y(0, 3)
    ag_x(1, 0)
    ag_x(1, 1)
    ag_sib(0, 2)
    out_chunk(2)
    for r in ro:
        r.near_m()
    xfo.send(2)
    ag_far(0, 3)
    ro[0].relay_p()
    ro[0].relay_m()
    ag_y(1, 0)
    ag_x(1, 2)
    ag_sib(0, 3)
    out_chunk(3)
    xfo.send(3)
    ag_y(1, 1)
    ag_x(1, 3)
    ag_far(1, 0)
    ro[1].relay_p()
    ro[1].relay_m()

    def joined_grad(nb):
        for l in wo_loads[nb]:
            l.wait()
        row = wo_rows[nb]

        def step(r):
            rows = pl.ds(al(r * 384, 128), 384)
            acc = jnp.zeros((384, 256), F32)
            for j in range(4):
                w = wslot[pl.ds(row + (j // 2) * 256, 256), pl.ds((j % 2) * 768, 768)]
                acc = acc + nt(buf_a[j, pl.ds(r * 4, 4)].reshape(384, 768), w)
            g = acc.astype(BF16)
            if nb == 0:
                gh[rows, :] = g
            else:
                cols = pl.ds((nb - 1) * 256, 256)
                gproj[rows, pl.ds(768 + (nb - 1) * 256, 256)] = (
                    g.astype(F32) * slope[rows, cols]
                ).astype(BF16)

        loop(2, step)

    joined_grad(0)
    for l in wo_loads[3]:
        l.start()
    joined_grad(1)
    ag_far(1, 1)
    ag_y(1, 2)
    xfo.take(0)
    joined_grad(2)
    joined_grad(3)
    ag_far(1, 2)
    ag_y(1, 3)

    def win_load(j):
        return load(
            win.at[pl.ds(j * 768, 768), :], wslot.at[pl.ds((j % 2) * 768, 768)], 4 + j
        )

    win_load(0).start()
    win_load(1).start()

    def att_bwd(b):
        rows = pl.ds(b * 256, 256)
        for h in range(2):
            q = qkv[rows, pl.ds(h * 128, 128)]
            k = qkv[rows, pl.ds(256 + h * 128, 128)]
            v = qkv[rows, pl.ds(512 + h * 128, 128)]
            g = gh[rows, pl.ds(h * 128, 128)]
            p = pf[b * 2 + h]
            delta = jnp.sum(
                g.astype(F32) * heads[rows, pl.ds(h * 128, 128)].astype(F32),
                axis=-1, keepdims=True,
            )
            ds = (p * (nt(g, v) - delta) * SCALE).astype(BF16)
            gproj[rows, pl.ds(512 + h * 128, 128)] = tn(p.astype(BF16), g).astype(BF16)
            gproj[rows, pl.ds(h * 128, 128)] = nn(ds, k).astype(BF16)
            gproj[rows, pl.ds(256 + h * 128, 128)] = tn(ds, q).astype(BF16)

    att_bwd(0)
    att_bwd(1)
    att_bwd(2)
    xfo.take(1)

    ag_drain(0)

    def transposed(o):
        ag_sib(1, o)
        j = order[o]

        def step(i):
            block = buf_b[j, pl.ds(i * 4, 4)].reshape(384, 768)
            rows = pl.ds(al(i * 384, 128), 384)
            buf_a[j, :, :, :, rows] = jnp.transpose(block).reshape(8, 2, 48, 384)

        loop(2, step)

    def in_chunk(o):
        j = order[o]

        def step(i):
            h, n = i // 2, i % 2
            cols = pl.ds(al(n * 768, 128), 768)
            left_side = buf_a[j, pl.ds(h * 4, 4)].reshape(384, 768)
            cin[j * 2 + h, :, cols] = nn(left_side, gproj[:, cols]).astype(BF16)

        loop(4, step)

    transposed(0)
    in_chunk(0)
    for r in ri:
        r.far()
    xfi.send(0)
    ag_far(1, 3)
    transposed(1)
    in_chunk(1)
    ri[0].near_p()
    xfi.send(1)
    xfo.take(2)
    transposed(2)
    in_chunk(2)
    ri[0].near_m()
    xfi.send(2)
    transposed(3)
    in_chunk(3)
    xfi.send(3)
    xfo.take(3)
    ag_drain(1)

    def sib_copy(j):
        return remote(buf_b.at[j, :, cn], rs_sib.at[j], m_s.at[0], ms_r.at[j], d_sib)

    def normed_grad(j):
        win_load(j).wait()
        base = (j % 2) * 768

        def step(i):
            h, n = i // 3, i % 3
            rows = pl.ds(al(h * 384, 128), 384)
            w = wslot[pl.ds(al(base + n * 256, 256), 256), :]
            t = nt(gproj[rows, :], w).astype(BF16)
            cols = pl.ds(al(n * 256, 128), 256)
            buf_b[j, pl.ds(h * 4, 4), :, :, cols] = t.reshape(4, 2, 48, 256)

        loop(6, step)
        sib_copy(j).start()
        if j < 2:
            win_load(j + 2).start()

    y_out = ((pair_p, d_yp), (pair_m, d_ym), (pair_2, d_y2))

    def sib_sum(j):
        sib_copy(j).wait_recv()

        def step(i):
            buf_b[j, i, c] = (buf_b[j, i, c].astype(F32) + rs_sib[j, i].astype(F32)).astype(BF16)

        loop(8, step)
        for i, (at, d) in enumerate(y_out):
            remote(buf_b.at[j, at, c], rs_y.at[j, i], m_s.at[1], my_r.at[j], d).start()

    def x_copy(j):
        return remote(ss_x.at[j], rs_x.at[j], m_s.at[2], mx_r.at[j], d_xn)

    def y_sum(j):
        remote(rs_y.at[j], rs_y.at[j], m_s.at[1], my_r.at[j], d_yp).wait_recv()

        def total(side):
            acc = buf_b[j, 2 * y + side, c].astype(F32)
            for i in range(3):
                acc = acc + rs_y[j, i, side].astype(F32)
            return acc

        ss_x[j] = total(xn).astype(BF16)
        x_copy(j).start()
        gn[:, pl.ds(j * 768, 768)] = total(xl)

    def x_sum(j):
        x_copy(j).wait_recv()
        cols = pl.ds(j * 768, 768)
        gn[:, cols] = gn[:, cols] + rs_x[j].astype(F32)

    normed_grad(0)
    ri[0].relay_p()
    ri[0].relay_m()
    ri[1].near_p()
    ri[1].near_m()
    normed_grad(1)
    sib_sum(0)
    co[0].send()
    co[1].send()
    normed_grad(2)
    ri[1].relay_p()
    ri[1].relay_m()
    ri[2].near_p()
    ri[2].near_m()
    sib_sum(1)
    normed_grad(3)
    ri[2].relay_p()
    ri[2].relay_m()
    fo.relay_p()
    fo.relay_m()
    sib_sum(2)
    xfi.take(0)
    sib_sum(3)
    y_sum(0)
    xfi.take(1)
    y_sum(1)
    xfi.take(2)
    y_sum(2)
    y_sum(3)
    xfi.take(3)
    co[0].finish()
    co[1].finish()
    ci[0].send()
    for j in range(4):
        x_sum(j)
    xh_v = xhat[...]
    sg = gn[...] * gain[...]
    m1 = jnp.mean(sg, axis=-1, keepdims=True)
    m2 = jnp.mean(sg * xh_v, axis=-1, keepdims=True)
    own_tok[...] = (
        own_dout[...].astype(F32) + (sg - m1 - xh_v * m2) * rstd_ref[:, :1]
    ).astype(BF16)
    st_g = load(own_tok, ig, 0)
    st_g.start()
    ci[1].send()
    ci[0].finish()
    ci[1].finish()
    ci[2].send()
    xfo.finish()
    st_o = load(rxo, gwout, 1)
    st_o.start()
    fi.relay_p()
    fi.relay_m()
    st_i = [
        load(rxi.at[pl.ds(a, n)], gwin.at[pl.ds(a, n)], 2 + i)
        for i, (a, n) in enumerate(((0, 4 * HI), (4 * HI, 2 * HI), (base_i, XI)))
    ]
    st_i[0].start()
    xfi.finish()
    st_i[2].start()
    ci[2].finish()
    st_i[1].start()
    for r in ro + ri + [fo, fi] + co + ci + [xfo, xfi]:
        r.drain()
    for b, i in ((rs_sib, 0), (rs_y, 1), (rs_x, 2)):
        remote(b, b, m_s.at[i], mx_r.at[0], d_sib).wait_send()
    st_o.wait()
    st_g.wait()
    for st in st_i:
        st.wait()


def body(block_input_tokens, norm_gain_vector, w_in, w_out, saved_qkv, mlp_pre, output_gradient):
    hbm = pl.BlockSpec(memory_space=pl.ANY)
    sem = pltpu.SemaphoreType.DMA
    v = pltpu.VMEM
    ig, gwin, gwout = pl.pallas_call(
        kernel,
        name="block_backward",
        out_shape=(
            jax.ShapeDtypeStruct((48, 3072), BF16),
            jax.ShapeDtypeStruct((384, 1536), BF16),
            jax.ShapeDtypeStruct((1024, 384), BF16),
        ),
        in_specs=[hbm, pl.BlockSpec(memory_space=pltpu.VMEM), hbm, hbm, hbm, hbm, hbm],
        out_specs=(hbm, hbm, hbm),
        scratch_shapes=[
            v((4, 8, 2, 48, 768), BF16), v((4, 8, 2, 48, 768), BF16), v((768, 768), BF16),
            v((768, 768), BF16), v((768, 768), F32), v((6, 256, 256), F32),
            v((768, 256), BF16), v((1024, 768), BF16), v((768, 256), BF16),
            v((768, 1536), BF16), v((1536, 1536), BF16), v((8, 1024, 384), BF16),
            v((8, 384, 1536), BF16),
            v((NSO, 6, 2, HO, 384), BF16), v((NSI, 6, 2, HI, 1536), BF16),
            v((6, XO // 2, 384), BF16), v((6, XI // 2, 1536), BF16),
            v((4, XO, 384), BF16), v((4, XI, 1536), BF16),
            v((1024, 384), BF16), v((384, 1536), BF16), v((4, 8, 48, 768), BF16),
            v((4, 3, 2, 48, 768), BF16), v((4, 48, 768), BF16), v((4, 48, 768), BF16),
            v((48, 3072), F32), v((48, 3072), F32), v((48, 3072), BF16),
            v((48, 3072), BF16), v((48, 128), F32),
            sem((16,)), sem((2, 2)), sem((2, 4, 4)),
            sem((NSO, 6)), sem((NSO, 6)), sem((NSI, 6)), sem((NSI, 6)),
            sem((6,)), sem((6,)), sem((6,)), sem((6,)),
            sem((NSO, 2)), sem((NSO, 2)), sem((NSI, 2)), sem((NSI, 2)),
            sem((4,)), sem((4,)), sem((4,)), sem((4,)), sem((3,)), sem((4,)), sem((4,)), sem((4,)),
        ],
        compiler_params=pltpu.CompilerParams(
            collective_id=0, has_side_effects=True, vmem_limit_bytes=63 << 20
        ),
    )(
        block_input_tokens, norm_gain_vector.reshape(1, -1), w_in, w_out, saved_qkv, mlp_pre,
        output_gradient,
    )
    return ig, gwin.astype(F32), gwout.astype(F32)


def solution(mesh):
    placed = (
        P(("dp", "mp"), None),
        P(),
        P(None, "mp"),
        P("mp", None),
        P("dp", "mp"),
        P("dp", "mp"),
        P(("dp", "mp"), None),
    )
    return jax.shard_map(
        body,
        mesh=mesh,
        in_specs=placed,
        out_specs=(P(("dp", "mp"), None), P("dp", "mp"), P("mp", "dp")),
        check_vma=False,
    )
```

```python
import functools

import jax
import jax.numpy as jnp
from jax import lax
from jax.experimental import pallas as pl
from jax.experimental.pallas import tpu as pltpu
from jax.sharding import PartitionSpec as P

HD = 128
F32 = jnp.float32
BF16 = jnp.bfloat16
SCALE = HD ** (-0.5)
MESH = pl.DeviceIdType.MESH
NSO, HO, XO = 3, 128, 256
BLOCKS = (3, 4, 5, 2, 0, 1)


def nt(a, b):
    return lax.dot_general(a, b, (((1,), (1,)), ((), ())), preferred_element_type=F32)


def nn(a, b):
    return lax.dot_general(a, b, (((1,), (0,)), ((), ())), preferred_element_type=F32)


def tn(a, b):
    return lax.dot_general(a, b, (((0,), (0,)), ((), ())), preferred_element_type=F32)


def loop(n, fn):
    def step(i, carry):
        fn(i)
        return carry

    if n == 1:
        fn(0)
    else:
        lax.fori_loop(0, n, step, 0)


def al(v, m):
    return pl.multiple_of(v, m)


def kernel(
    tok, gain_hbm, win, wout, qkv_hbm, pre_hbm, dout,
    ig, gwin, gwout,
    buf_a, buf_b, qkv, pre, slope, pf, heads, joined_t, gh, gproj, gp2, wslot, cout, cin,
    rzo, rzi, rfo, x1o, rxo, rxi, nsend, rs_sib, rs_y, rs_x, ss_x, xhat, gn, gain,
    own_tok, own_dout, rstd_ref,
    lsem, ag_s, ag_r, zo_s, zo_r, zi_s, zi_r, fo_s, fo_r, xo_s, xo_r,
    x1o_s, x1o_r, gx_s, gx_r, nx_s, m_s, ms_r, my_r, mx_r,
):
    dp = lax.axis_index("dp")
    mp = lax.axis_index("mp")
    z = dp // 2
    xh = dp % 2
    y = mp // 4
    xl = (mp // 2) % 2
    c = mp % 2
    zp, zm, z2 = (z + 1) % 4, (z + 3) % 4, (z + 2) % 4
    yp, ym, y2 = (y + 1) % 4, (y + 3) % 4, (y + 2) % 4
    xn, cn, xo = 1 - xl, 1 - c, 1 - xh

    def m_of(yy, xx, cc):
        return yy * 4 + xx * 2 + cc

    d_sib = (dp, m_of(y, xl, cn))
    d_xn = (dp, m_of(y, xn, c))
    d_yp = (dp, m_of(yp, xl, c))
    d_ym = (dp, m_of(ym, xl, c))
    d_y2 = (dp, m_of(y2, xl, c))
    d_zp = (zp * 2 + xh, mp)
    d_zm = (zm * 2 + xh, mp)
    d_xo = (z * 2 + xo, mp)
    friends = (d_sib, d_xn, d_yp, d_ym, d_y2, d_zp, d_zm, d_xo)

    def load(src, dst, i):
        return pltpu.make_async_copy(src, dst, lsem.at[i])

    own = 2 * y + xl
    order = (z2, zp, zm, z)
    l_dout = load(dout, own_dout, 12)
    l_tok = load(tok, own_tok, 0)
    l_gain = load(gain_hbm, gain, 1)
    l_qkv = load(qkv_hbm, qkv, 2)
    l_pre = load(pre_hbm, pre, 3)
    for l in (l_dout, l_tok, l_gain, l_qkv, l_pre):
        l.start()

    def wout_loads(nb, row):
        return [
            load(
                wout.at[pl.ds(nb * 256, 256), pl.ds(h * 1536, 1536)],
                wslot.at[pl.ds(row + h * 256, 256)],
                4 + nb * 2 + h,
            )
            for h in range(2)
        ]

    wo_rows = (0, 0, 512, 1024)
    wo_loads = [wout_loads(nb, wo_rows[nb]) for nb in range(4)]
    for nb in range(1, 4):
        for l in wo_loads[nb]:
            l.start()

    barrier = pltpu.get_barrier_semaphore()
    for d in friends:
        pl.semaphore_signal(barrier, inc=1, device_id=d, device_id_type=MESH)
    pl.semaphore_wait(barrier, len(friends))

    def remote(src, dst, s, r, d):
        return pltpu.make_async_remote_copy(
            src_ref=src, dst_ref=dst, send_sem=s, recv_sem=r, device_id=d, device_id_type=MESH
        )

    bufs = (buf_a, buf_b)
    pair, pair_p, pair_m, pair_2 = (pl.ds(2 * v, 2) for v in (y, yp, ym, y2))
    full = tuple((o, slice(None)) for o in range(4))
    chunks = (((0, pl.ds(0, 384)), (0, pl.ds(384, 384))) + full[1:], full)

    def ag_copy(w, k, kind, at, core, d):
        o, cols = chunks[w][k]
        b = bufs[w].at[order[o], at, core, :, cols]
        sent = ag_s.at[w, 0 if kind == 0 else 1]
        return remote(b, b, sent, ag_r.at[w, k, kind], d)

    def ag_sx(w, k):
        ag_copy(w, k, 0, own, c, d_xn).start()

    def ag_sy(w, k):
        ag_copy(w, k, 1, own, c, d_yp).start()
        ag_copy(w, k, 1, own, c, d_ym).start()

    def ag_x(w, k):
        ag_copy(w, k, 0, 2 * y + xn, c, d_xn).wait_recv()
        at = 2 * y + xn if w == 0 and k < 2 else pair
        ag_copy(w, k, 1, at, c, d_yp).start()
        ag_copy(w, k, 1, at, c, d_ym).start()
        ag_copy(w, k, 3, pair, c, d_sib).start()

    def ag_y(w, k):
        ag_copy(w, k, 1, pl.ds(0, 4), c, d_yp).wait_recv()
        ag_copy(w, k, 2, 2 * ym, c, d_yp).start()
        ag_copy(w, k, 2, 2 * yp + 1, c, d_ym).start()
        ag_copy(w, k, 3, pair_m, c, d_sib).start()
        ag_copy(w, k, 3, pair_p, c, d_sib).start()

    def ag_far(w, k):
        ag_copy(w, k, 2, pair_2, c, d_yp).wait_recv()
        ag_copy(w, k, 3, pair_2, c, d_sib).start()

    def ag_sib(w, k):
        ag_copy(w, k, 3, slice(None), cn, d_sib).wait_recv()

    def ag_drain(w):
        for i, b in enumerate((bufs[w].at[:, own, c], bufs[w].at[:, pl.ds(0, 7)])):
            remote(b, b, ag_s.at[w, i], ag_r.at[w, 0, 0], d_sib).wait_send()

    l_dout.wait()
    for o in range(4):
        buf_a[order[o], own, c] = own_dout[:, pl.ds(al(order[o] * 768, 128), 768)]
    ag_sx(0, 0)
    ag_sy(0, 0)
    ag_sx(0, 1)
    ag_sy(0, 1)
    ag_sx(0, 2)
    ag_sx(0, 3)
    ag_sx(0, 4)

    def layer_norm():
        l_tok.wait()
        l_gain.wait()
        x = own_tok[...].astype(F32)
        center = jnp.mean(x, axis=-1, keepdims=True)
        spread = jnp.mean((x - center) ** 2, axis=-1, keepdims=True)
        rstd = 1.0 / jnp.sqrt(spread + 1e-06)
        xhat[...] = (x - center) * rstd
        rstd_ref[...] = jnp.broadcast_to(rstd, rstd_ref.shape)
        for o in range(4):
            for half, dst in ((xh, buf_b.at[o, own, c, :, pl.ds(0, 384)]), (xo, nsend.at[o])):
                cols = pl.ds(al(o * 768 + half * 384, 128), 384)
                dst[...] = (xhat[:, cols] * gain[:, cols]).astype(BF16)
            nx_copy(o).start()

    def nx_copy(o):
        dst = buf_b.at[o, own, c, :, pl.ds(384, 384)]
        return remote(nsend.at[o], dst, nx_s.at[0], nx_s.at[1], d_xo)

    def nx_all():
        b = buf_b.at[:, own, c, :, pl.ds(384, 384)]
        return remote(nsend, b, nx_s.at[0], nx_s.at[1], d_xo)

    def nx_take():
        nx_all().wait_recv()
        for o in range(4):
            ag_sx(1, o)

    def att_fwd(b):
        rows = pl.ds(b * 256, 256)
        for h in range(2):
            q = qkv[rows, pl.ds(h * 128, 128)]
            k = qkv[rows, pl.ds(256 + h * 128, 128)]
            v = qkv[rows, pl.ds(512 + h * 128, 128)]
            s = nt(q, k) * SCALE
            e = jnp.exp(s - jnp.max(s, axis=-1, keepdims=True))
            p = e / jnp.sum(e, axis=-1, keepdims=True)
            pf[b * 2 + h] = p
            out = nn(p.astype(BF16), v)
            heads[rows, pl.ds(h * 128, 128)] = out.astype(BF16)
            joined_t[pl.ds(h * 128, 128), rows] = jnp.transpose(out).astype(BF16)

    def gelu(t):
        rows = pl.ds(al(t * 128, 128), 128)
        v = pre[rows, :].astype(F32)
        cumul = 0.5 * (1.0 + lax.erf(v * 0.7071067811865476))
        joined_t[pl.ds(256, 768), rows] = jnp.transpose(v * cumul).astype(BF16)
        dens = jnp.exp(-0.5 * v * v) * 0.3989422804014327
        slope[rows, :] = cumul + v * dens

    l_pre.wait()
    gelu(0)
    gelu(1)
    ag_x(0, 0)
    l_qkv.wait()
    att_fwd(0)
    ag_x(0, 1)
    att_fwd(1)
    ag_y(0, 0)
    att_fwd(2)
    ag_x(0, 2)
    gelu(2)
    ag_y(0, 1)
    ag_x(0, 3)
    gelu(3)
    gelu(4)
    gelu(5)
    ag_far(0, 0)
    layer_norm()
    ag_y(0, 2)
    ag_far(0, 1)
    ag_x(0, 4)
    ag_sib(0, 0)

    class Ring:
        def __init__(self, src, rbuf, ssem, rsem, add):
            self.src, self.rbuf, self.ssem, self.rsem, self.add = src, rbuf, ssem, rsem, add
            self.sent = []

        def send(self, i, src, d):
            cp = remote(src, self.rbuf.at[i], self.ssem.at[i], self.rsem.at[i], d)
            cp.start()
            self.sent.append(cp)

        def wait(self, i):
            b = self.rbuf.at[i]
            remote(b, b, self.ssem.at[i], self.rsem.at[i], d_zp).wait_recv()

        def far(self):
            self.send(0, self.src(z2, 1), d_zp)
            self.send(1, self.src(z2, 0), d_zm)

        def far_block(self, h):
            for i, d in ((0, d_zp), (1, d_zm)):
                cp = remote(
                    self.src(z2, 1 - i).at[h], self.rbuf.at[i, h],
                    self.ssem.at[i], self.rsem.at[i], d,
                )
                cp.start()
                if h == 0:
                    b = self.rbuf.at[i]
                    self.sent.append(remote(b, b, self.ssem.at[i], self.rsem.at[i], d))

        def near_p(self):
            self.send(2, self.src(zp, 0), d_zp)

        def near_m(self):
            self.send(3, self.src(zm, 1), d_zm)

        def relay_p(self):
            self.wait(0)
            self.add(self.rbuf.at[0], self.src(zp, 1))
            self.send(4, self.rbuf.at[0], d_zp)

        def relay_m(self):
            self.wait(1)
            self.add(self.rbuf.at[1], self.src(zm, 0))
            self.send(5, self.rbuf.at[1], d_zm)

        def arrived(self):
            for i in (2, 3, 4, 5):
                self.wait(i)

        def drain(self):
            for cp in self.sent:
                cp.wait_send()

    def adder(lead, height, tile):
        def add(dst, src):
            def step(i):
                rows = pl.ds(al(i * tile, tile), tile)
                for at in lead:
                    dst[at + (rows, slice(None))] = (
                        dst[at + (rows, slice(None))].astype(F32)
                        + src[at + (rows, slice(None))].astype(F32)
                    ).astype(BF16)

            loop(height // tile, step)

        return add

    def z_first(part, base, height):
        return lambda zz, half: part.at[pl.ds(zz * 2, 2), pl.ds(base + half * height, height), :]

    def x_first(part, base, height):
        return lambda zz, half: part.at[zz * 2 + xh, pl.ds(base + half * height, height), :]

    both = ((0,), (1,))
    ro = [
        Ring(z_first(cout, s * 2 * HO, HO), rzo.at[s], zo_s.at[s], zo_r.at[s], adder(both, HO, 64))
        for s in range(NSO)
    ]
    def in_src(n):
        return lambda zz, half: cin.at[n, zz, pl.ds(half * 192, 192), :]

    rn = [
        Ring(in_src(n), rzi.at[n], zi_s.at[n], zi_r.at[n], adder(((),), 192, 96)) for n in range(6)
    ]
    base_o = 1024 - XO
    fo = Ring(x_first(cout, base_o, XO // 2), rfo, fo_s, fo_r, adder(((),), XO // 2, 64))

    class Cross:
        def __init__(self, ring, part, rx, ssem, rsem, base, height, tile):
            self.ring, self.part, self.rx = ring, part, rx
            self.ssem, self.rsem = ssem, rsem
            self.base, self.height, self.tile = base, height, tile
            self.sent = []

        def send(self):
            self.ring.arrived()
            r = self.ring.rbuf
            for half, (a, b) in enumerate(((2, 5), (3, 4))):
                off = self.base + half * self.height

                def step(i, a=a, b=b, off=off):
                    rows = pl.ds(al(i * self.tile, self.tile), self.tile)
                    prow = pl.ds(al(off + i * self.tile, self.tile), self.tile)
                    r[a, xo, rows, :] = (
                        r[a, xo, rows, :].astype(F32)
                        + r[b, xo, rows, :].astype(F32)
                        + self.part[z * 2 + xo, prow, :].astype(F32)
                    ).astype(BF16)

                loop(self.height // self.tile, step)
                cp = remote(
                    r.at[a, xo], self.rx.at[pl.ds(off, self.height), :],
                    self.ssem.at[half], self.rsem.at[half], d_xo,
                )
                cp.start()
                self.sent.append(cp)

        def finish(self):
            r = self.ring.rbuf
            for half, (a, b) in enumerate(((2, 5), (3, 4))):
                off = self.base + half * self.height
                dst = self.rx.at[pl.ds(off, self.height), :]
                remote(dst, dst, self.ssem.at[half], self.rsem.at[half], d_xo).wait_recv()

                def step(i, a=a, b=b, off=off):
                    rows = pl.ds(al(i * self.tile, self.tile), self.tile)
                    prow = pl.ds(al(off + i * self.tile, self.tile), self.tile)
                    self.rx[prow, :] = (
                        r[a, xh, rows, :].astype(F32)
                        + r[b, xh, rows, :].astype(F32)
                        + self.part[z * 2 + xh, prow, :].astype(F32)
                        + self.rx[prow, :].astype(F32)
                    ).astype(BF16)

                loop(self.height // self.tile, step)

        def drain(self):
            for cp in self.sent:
                cp.wait_send()

    class First:
        def __init__(self, ring, part, x1, rx, ssem, rsem, base, height, tile):
            self.ring, self.part, self.x1, self.rx = ring, part, x1, rx
            self.ssem, self.rsem = ssem, rsem
            self.base, self.height, self.tile = base, height, tile

        def copy(self, o):
            return remote(
                self.part.at[order[o] * 2 + xo, pl.ds(self.base, self.height), :],
                self.x1.at[o], self.ssem.at[o], self.rsem.at[o], d_xo,
            )

        def send(self, o):
            self.copy(o).start()

        def take(self, o):
            self.copy(o).wait_recv()

            def step(i):
                rows = pl.ds(al(i * self.tile, self.tile), self.tile)
                prow = pl.ds(al(self.base + i * self.tile, self.tile), self.tile)
                mine = order[o] * 2 + xh
                self.part[mine, prow, :] = (
                    self.part[mine, prow, :].astype(F32) + self.x1[o, rows, :].astype(F32)
                ).astype(BF16)

            loop(self.height // self.tile, step)
            if o < 3:
                (self.ring.far, self.ring.near_p, self.ring.near_m)[o]()

        def finish(self):
            self.ring.arrived()
            r = self.ring.rbuf
            half_rows = self.height // 2
            for half, (a, b) in enumerate(((2, 5), (3, 4))):
                off = self.base + half * half_rows

                def step(i, a=a, b=b, off=off):
                    rows = pl.ds(al(i * self.tile, self.tile), self.tile)
                    prow = pl.ds(al(off + i * self.tile, self.tile), self.tile)
                    self.rx[prow, :] = (
                        r[a, rows, :].astype(F32)
                        + r[b, rows, :].astype(F32)
                        + self.part[z * 2 + xh, prow, :].astype(F32)
                    ).astype(BF16)

                loop(half_rows // self.tile, step)

        def drain(self):
            for o in range(4):
                self.copy(o).wait_send()

    co = [
        Cross(ro[s], cout, rxo, xo_s.at[s], xo_r.at[s], s * 2 * HO, HO, 64) for s in range(NSO)
    ]
    xfo = First(fo, cout, x1o, rxo, x1o_s, x1o_r, base_o, XO, 64)

    def out_half(h):
        j = order[0]

        def step(r):
            rows = pl.ds(al(r * 256, 256), 256)
            right_side = buf_a[j, :, :, :, pl.ds(h * 384, 384)].reshape(768, 384)
            cout[j * 2 + h, rows, :] = nn(joined_t[rows, :], right_side).astype(BF16)

        loop(4, step)

    def out_chunk(o):
        j = order[o]

        def step(r):
            rows = pl.ds(al(r * 256, 256), 256)
            t = nn(joined_t[rows, :], buf_a[j].reshape(768, 768)).astype(BF16)
            cout[j * 2, rows, :] = t[:, :384]
            cout[j * 2 + 1, rows, :] = t[:, 384:]

        loop(4, step)

    out_half(0)
    for r in ro:
        r.far_block(0)
    ag_sib(0, 1)
    out_half(1)
    for r in ro:
        r.far_block(1)
    nx_take()
    xfo.send(0)
    ag_far(0, 2)
    ag_y(0, 3)
    ag_sib(0, 2)
    out_chunk(1)
    for r in ro:
        r.near_p()
    xfo.send(1)
    ag_far(0, 3)
    ag_y(0, 4)
    ag_x(1, 0)
    ag_sib(0, 3)
    out_chunk(2)
    for r in ro:
        r.near_m()
    xfo.send(2)
    ag_far(0, 4)
    ag_x(1, 1)
    ag_sib(0, 4)
    out_chunk(3)
    xfo.send(3)
    ag_y(1, 0)
    ro[0].relay_p()
    ro[0].relay_m()
    ag_x(1, 2)
    ag_y(1, 1)
    ag_x(1, 3)
    ag_far(1, 0)
    ro[1].relay_p()
    ro[1].relay_m()

    def joined_grad(nb):
        for l in wo_loads[nb]:
            l.wait()
        row = wo_rows[nb]

        def step(r):
            rows = pl.ds(al(r * 384, 128), 384)
            acc = jnp.zeros((384, 256), F32)
            for j in range(4):
                w = wslot[pl.ds(row + (j // 2) * 256, 256), pl.ds((j % 2) * 768, 768)]
                acc = acc + nt(buf_a[j, pl.ds(r * 4, 4)].reshape(384, 768), w)
            g = acc.astype(BF16)
            if nb == 0:
                gh[rows, :] = g
            else:
                cols = pl.ds((nb - 1) * 256, 256)
                gproj[2 + nb, rows, :] = (g.astype(F32) * slope[rows, cols]).astype(BF16)

        loop(2, step)

    def gx_copy(n):
        return remote(gproj.at[n], gp2.at[n], gx_s, gx_r.at[n], d_xo)

    def gx_send(n):
        gx_copy(n).start()

    def gx_wait(n):
        gx_copy(n).wait_recv()

    joined_grad(1)
    gx_send(3)
    for l in wo_loads[0]:
        l.start()
    ag_far(1, 1)
    ag_y(1, 2)
    joined_grad(2)
    gx_send(4)
    xfo.take(0)
    joined_grad(3)
    gx_send(5)
    ag_far(1, 2)
    ag_y(1, 3)
    ro[2].relay_p()
    ro[2].relay_m()
    joined_grad(0)

    def win_load(j):
        return load(
            win.at[pl.ds(j * 768, 768), :], wslot.at[pl.ds((j % 2) * 768, 768)], 4 + j
        )

    win_load(0).start()
    win_load(1).start()

    def att_bwd(b):
        rows = pl.ds(b * 256, 256)
        for h in range(2):
            q = qkv[rows, pl.ds(h * 128, 128)]
            k = qkv[rows, pl.ds(256 + h * 128, 128)]
            v = qkv[rows, pl.ds(512 + h * 128, 128)]
            g = gh[rows, pl.ds(h * 128, 128)]
            p = pf[b * 2 + h]
            delta = jnp.sum(
                g.astype(F32) * heads[rows, pl.ds(h * 128, 128)].astype(F32),
                axis=-1, keepdims=True,
            )
            ds = (p * (nt(g, v) - delta) * SCALE).astype(BF16)
            gproj[2, rows, pl.ds(h * 128, 128)] = tn(p.astype(BF16), g).astype(BF16)
            gproj[0, rows, pl.ds(h * 128, 128)] = nn(ds, k).astype(BF16)
            gproj[1, rows, pl.ds(h * 128, 128)] = tn(ds, q).astype(BF16)

    att_bwd(0)
    att_bwd(1)
    att_bwd(2)
    gx_send(2)
    gx_send(0)
    gx_send(1)
    ag_far(1, 3)
    xfo.take(1)

    ag_drain(0)

    def transposed(o):
        ag_sib(1, o)
        j = order[o]

        def step(i):
            block = buf_b[j, pl.ds(i * 4, 4)].reshape(384, 768)
            rows = pl.ds(al(i * 384, 128), 384)
            buf_a[j, :, :, :, rows] = jnp.transpose(block).reshape(8, 2, 48, 384)

        loop(2, step)

    def in_block(n, o):
        j = order[o]
        left_own = buf_a[j, pl.ds(0, 4)].reshape(384, 768)
        left_other = buf_a[j, pl.ds(4, 4)].reshape(384, 768)
        cin[n, j] = (nn(left_own, gproj[n]) + nn(left_other, gp2[n])).astype(BF16)

    def in_finish(n):
        rn[n].arrived()
        r = rzi.at[n]
        for half, (a, b) in enumerate(((2, 5), (3, 4))):
            rows = pl.ds(half * 192, 192)
            rxi[n, rows, :] = (
                r[a].astype(F32) + r[b].astype(F32) + cin[n, z, rows, :].astype(F32)
            ).astype(BF16)

    transposed(0)
    transposed(1)
    transposed(2)
    transposed(3)
    ag_drain(1)
    gx_wait(3)
    in_block(3, 0)
    rn[3].far()
    in_block(3, 1)
    rn[3].near_p()
    in_block(3, 2)
    rn[3].near_m()
    in_block(3, 3)
    xfo.take(2)
    xfo.take(3)

    def sib_copy(j):
        return remote(buf_b.at[j, :, cn], rs_sib.at[j], m_s.at[0], ms_r.at[j], d_sib)

    def normed_grad(j):
        win_load(j).wait()
        base = (j % 2) * 768

        def step(i):
            h, n = i // 3, i % 3
            rows = pl.ds(al(h * 384, 128), 384)
            w = wslot[pl.ds(al(base + n * 256, 256), 256), :]
            acc = nt(gproj[0, rows, :], w[:, :256])
            for k in range(1, 6):
                acc = acc + nt(gproj[k, rows, :], w[:, k * 256 : k * 256 + 256])
            t = acc.astype(BF16)
            cols = pl.ds(al(n * 256, 128), 256)
            buf_b[j, pl.ds(h * 4, 4), :, :, cols] = t.reshape(4, 2, 48, 256)

        loop(6, step)
        sib_copy(j).start()
        if j < 2:
            win_load(j + 2).start()

    y_out = ((pair_p, d_yp), (pair_m, d_ym), (pair_2, d_y2))

    def sib_sum(j):
        sib_copy(j).wait_recv()

        def step(i):
            buf_b[j, i, c] = (buf_b[j, i, c].astype(F32) + rs_sib[j, i].astype(F32)).astype(BF16)

        loop(8, step)
        for i, (at, d) in enumerate(y_out):
            remote(buf_b.at[j, at, c], rs_y.at[j, i], m_s.at[1], my_r.at[j], d).start()

    def x_copy(j):
        return remote(ss_x.at[j], rs_x.at[j], m_s.at[2], mx_r.at[j], d_xn)

    def y_sum(j):
        remote(rs_y.at[j], rs_y.at[j], m_s.at[1], my_r.at[j], d_yp).wait_recv()

        def total(side):
            acc = buf_b[j, 2 * y + side, c].astype(F32)
            for i in range(3):
                acc = acc + rs_y[j, i, side].astype(F32)
            return acc

        ss_x[j] = total(xn).astype(BF16)
        x_copy(j).start()
        gn[:, pl.ds(j * 768, 768)] = total(xl)

    def x_sum(j):
        x_copy(j).wait_recv()
        cols = pl.ds(j * 768, 768)
        gn[:, cols] = gn[:, cols] + rs_x[j].astype(F32)

    normed_grad(0)
    gx_wait(4)
    in_block(4, 0)
    rn[4].far()
    in_block(4, 1)
    rn[4].near_p()
    in_block(4, 2)
    rn[4].near_m()
    in_block(4, 3)
    rn[3].relay_p()
    rn[3].relay_m()
    normed_grad(1)
    sib_sum(0)
    fo.relay_p()
    fo.relay_m()
    gx_wait(5)
    in_block(5, 0)
    rn[5].far()
    in_block(5, 1)
    rn[5].near_p()
    in_block(5, 2)
    rn[5].near_m()
    in_block(5, 3)
    rn[4].relay_p()
    rn[4].relay_m()
    normed_grad(2)
    sib_sum(1)
    co[0].send()
    co[1].send()
    y_sum(0)
    gx_wait(2)
    in_block(2, 0)
    rn[2].far()
    in_block(2, 1)
    rn[2].near_p()
    in_block(2, 2)
    rn[2].near_m()
    in_block(2, 3)
    rn[5].relay_p()
    rn[5].relay_m()
    normed_grad(3)
    sib_sum(2)
    y_sum(1)
    co[2].send()
    in_finish(3)
    gx_wait(0)
    in_block(0, 0)
    rn[0].far()
    in_block(0, 1)
    rn[0].near_p()
    in_block(0, 2)
    rn[0].near_m()
    in_block(0, 3)
    rn[2].relay_p()
    rn[2].relay_m()
    sib_sum(3)
    y_sum(2)
    in_finish(4)
    xfo.finish()
    y_sum(3)
    gx_wait(1)
    in_block(1, 0)
    rn[1].far()
    in_block(1, 1)
    rn[1].near_p()
    in_block(1, 2)
    rn[1].near_m()
    in_block(1, 3)
    rn[0].relay_p()
    rn[0].relay_m()
    in_finish(5)
    rn[1].relay_p()
    rn[1].relay_m()
    in_finish(2)
    co[0].finish()
    co[1].finish()
    co[2].finish()
    st_o = load(rxo, gwout, 1)
    st_o.start()
    in_finish(0)
    for j in range(4):
        x_sum(j)
    xh_v = xhat[...]
    sg = gn[...] * gain[...]
    m1 = jnp.mean(sg, axis=-1, keepdims=True)
    m2 = jnp.mean(sg * xh_v, axis=-1, keepdims=True)
    own_tok[...] = (
        own_dout[...].astype(F32) + (sg - m1 - xh_v * m2) * rstd_ref[:, :1]
    ).astype(BF16)
    st_g = load(own_tok, ig, 0)
    st_g.start()
    in_finish(1)
    st_i = [load(rxi.at[n], gwin.at[:, pl.ds(n * 256, 256)], 2 + n) for n in range(6)]
    for st in st_i:
        st.start()
    gx_all = remote(gproj, gp2, gx_s, gx_r.at[0], d_xo)
    gx_all.wait_send()
    nx_all().wait_send()
    for r in ro + rn + [fo] + co + [xfo]:
        r.drain()
    for b, i in ((rs_sib, 0), (rs_y, 1), (rs_x, 2)):
        remote(b, b, m_s.at[i], mx_r.at[0], d_sib).wait_send()
    st_o.wait()
    st_g.wait()
    for st in st_i:
        st.wait()


def widen(ig, gwin, gwout, ig_out, gwin_out, gwout_out, tg, ti, to, fi, fo, isem, osem):
    def copies(k):
        if k == 8:
            return ig, tg, tg, ig_out
        if k < 4:
            at = pl.ds(k * 96, 96)
            return gwin.at[at], ti.at[at], fi.at[at], gwin_out.at[at]
        at = pl.ds((k - 4) * 256, 256)
        return gwout.at[at], to.at[at], fo.at[at], gwout_out.at[at]

    ins = [pltpu.make_async_copy(copies(k)[0], copies(k)[1], isem.at[k]) for k in range(9)]
    outs = [pltpu.make_async_copy(copies(k)[2], copies(k)[3], osem.at[k]) for k in range(9)]
    for cp in ins:
        cp.start()
    for k in range(9):
        ins[k].wait()
        if k < 8:
            src, dst = copies(k)[1:3]
            dst[...] = src[...].astype(F32)
        outs[k].start()
    for cp in outs:
        cp.wait()


def body(block_input_tokens, norm_gain_vector, w_in, w_out, saved_qkv, mlp_pre, output_gradient):
    hbm = pl.BlockSpec(memory_space=pl.ANY)
    sem = pltpu.SemaphoreType.DMA
    v = pltpu.VMEM
    ig, gwin, gwout = pl.pallas_call(
        kernel,
        name="block_backward",
        out_shape=(
            jax.ShapeDtypeStruct((48, 3072), BF16),
            jax.ShapeDtypeStruct((384, 1536), BF16),
            jax.ShapeDtypeStruct((1024, 384), BF16),
        ),
        in_specs=[hbm] * 7,
        out_specs=(hbm, hbm, hbm),
        scratch_shapes=[
            v((4, 8, 2, 48, 768), BF16), v((4, 8, 2, 48, 768), BF16), v((768, 768), BF16),
            v((768, 768), BF16), v((768, 768), F32), v((6, 256, 256), F32),
            v((768, 256), BF16), v((1024, 768), BF16), v((768, 256), BF16),
            v((6, 768, 256), BF16), v((6, 768, 256), BF16), v((1536, 1536), BF16),
            v((8, 1024, 384), BF16), v((6, 4, 384, 256), BF16),
            v((NSO, 6, 2, HO, 384), BF16), v((6, 6, 192, 256), BF16),
            v((6, XO // 2, 384), BF16), v((4, XO, 384), BF16),
            v((1024, 384), BF16), v((6, 384, 256), BF16), v((4, 48, 384), BF16),
            v((4, 8, 48, 768), BF16),
            v((4, 3, 2, 48, 768), BF16), v((4, 48, 768), BF16), v((4, 48, 768), BF16),
            v((48, 3072), F32), v((48, 3072), F32), v((1, 3072), F32), v((48, 3072), BF16),
            v((48, 3072), BF16), v((48, 128), F32),
            sem((16,)), sem((2, 2)), sem((2, 5, 4)),
            sem((NSO, 6)), sem((NSO, 6)), sem((6, 6)), sem((6, 6)), sem((6,)), sem((6,)),
            sem((NSO, 2)), sem((NSO, 2)),
            sem((4,)), sem((4,)), sem, sem((6,)), sem((2,)), sem((3,)), sem((4,)), sem((4,)), sem((4,)),
        ],
        compiler_params=pltpu.CompilerParams(
            collective_id=0, has_side_effects=True, vmem_limit_bytes=63 << 20
        ),
    )(
        block_input_tokens, norm_gain_vector.reshape(1, -1), w_in, w_out, saved_qkv, mlp_pre,
        output_gradient,
    )
    return pl.pallas_call(
        widen,
        name="widen",
        out_shape=(
            jax.ShapeDtypeStruct((48, 3072), BF16),
            jax.ShapeDtypeStruct((384, 1536), F32),
            jax.ShapeDtypeStruct((1024, 384), F32),
        ),
        in_specs=[hbm] * 3,
        out_specs=(hbm,) * 3,
        scratch_shapes=[
            v((48, 3072), BF16), v((384, 1536), BF16), v((1024, 384), BF16),
            v((384, 1536), F32), v((1024, 384), F32), sem((9,)), sem((9,)),
        ],
        compiler_params=pltpu.CompilerParams(vmem_limit_bytes=62 << 20),
    )(ig, gwin, gwout)


def solution(mesh):
    placed = (
        P(("dp", "mp"), None),
        P(),
        P(None, "mp"),
        P("mp", None),
        P("dp", "mp"),
        P("dp", "mp"),
        P(("dp", "mp"), None),
    )
    return jax.shard_map(
        body,
        mesh=mesh,
        in_specs=placed,
        out_specs=(P(("dp", "mp"), None), P("dp", "mp"), P("mp", "dp")),
        check_vma=False,
    )
```

```python
import functools

import jax
import jax.numpy as jnp
from jax import lax
from jax.experimental import pallas as pl
from jax.experimental.pallas import tpu as pltpu
from jax.sharding import PartitionSpec as P

HD = 128
F32 = jnp.float32
BF16 = jnp.bfloat16
SCALE = HD ** (-0.5)
MESH = pl.DeviceIdType.MESH
NSO, HO, XO = 3, 144, 160
BLOCKS = (3, 4, 5, 2, 0, 1)


def nt(a, b):
    return lax.dot_general(a, b, (((1,), (1,)), ((), ())), preferred_element_type=F32)


def nn(a, b):
    return lax.dot_general(a, b, (((1,), (0,)), ((), ())), preferred_element_type=F32)


def tn(a, b):
    return lax.dot_general(a, b, (((0,), (0,)), ((), ())), preferred_element_type=F32)


def loop(n, fn):
    def step(i, carry):
        fn(i)
        return carry

    if n == 1:
        fn(0)
    else:
        lax.fori_loop(0, n, step, 0)


def al(v, m):
    return pl.multiple_of(v, m)


def kernel(
    tok, gain_hbm, win, wout, qkv_hbm, pre_hbm, dout,
    ig, gwin, gwout,
    buf_a, buf_b, qkv, pre, slope, pf, heads, joined_t, gh, gproj, gp2, wslot, cout, cin,
    rzo, rzi, rfo, x1o, rxo, rxi, nsend, rs_sib, rs_y, rs_x, ss_x, xhat, gn, gain,
    own_tok, own_dout, rstd_ref,
    lsem, ag_s, ag_r, zo_s, zo_r, zi_s, zi_r, fo_s, fo_r, xo_s, xo_r,
    x1o_s, x1o_r, gx_s, gx_r, nx_s, m_s, ms_r, my_r, mx_r,
):
    dp = lax.axis_index("dp")
    mp = lax.axis_index("mp")
    z = dp // 2
    xh = dp % 2
    y = mp // 4
    xl = (mp // 2) % 2
    c = mp % 2
    zp, zm, z2 = (z + 1) % 4, (z + 3) % 4, (z + 2) % 4
    yp, ym, y2 = (y + 1) % 4, (y + 3) % 4, (y + 2) % 4
    xn, cn, xo = 1 - xl, 1 - c, 1 - xh

    def m_of(yy, xx, cc):
        return yy * 4 + xx * 2 + cc

    d_sib = (dp, m_of(y, xl, cn))
    d_xn = (dp, m_of(y, xn, c))
    d_yp = (dp, m_of(yp, xl, c))
    d_ym = (dp, m_of(ym, xl, c))
    d_y2 = (dp, m_of(y2, xl, c))
    d_zp = (zp * 2 + xh, mp)
    d_zm = (zm * 2 + xh, mp)
    d_xo = (z * 2 + xo, mp)
    friends = (d_sib, d_xn, d_yp, d_ym, d_y2, d_zp, d_zm, d_xo)

    def load(src, dst, i):
        return pltpu.make_async_copy(src, dst, lsem.at[i])

    own = 2 * y + xl
    order = (z2, zp, zm, z)
    l_dout = load(dout, own_dout, 12)
    l_tok = load(tok, own_tok, 0)
    l_gain = load(gain_hbm, gain, 1)
    l_qkv = load(qkv_hbm, qkv, 2)
    l_pre = load(pre_hbm, pre, 3)
    for l in (l_dout, l_tok, l_gain, l_qkv, l_pre):
        l.start()

    def wout_loads(nb, row):
        return [
            load(
                wout.at[pl.ds(nb * 256, 256), pl.ds(h * 1536, 1536)],
                wslot.at[pl.ds(row + h * 256, 256)],
                4 + nb * 2 + h,
            )
            for h in range(2)
        ]

    wo_rows = (0, 0, 512, 1024)
    wo_loads = [wout_loads(nb, wo_rows[nb]) for nb in range(4)]
    for nb in range(1, 4):
        for l in wo_loads[nb]:
            l.start()

    barrier = pltpu.get_barrier_semaphore()
    for d in friends:
        pl.semaphore_signal(barrier, inc=1, device_id=d, device_id_type=MESH)
    pl.semaphore_wait(barrier, len(friends))

    def remote(src, dst, s, r, d):
        return pltpu.make_async_remote_copy(
            src_ref=src, dst_ref=dst, send_sem=s, recv_sem=r, device_id=d, device_id_type=MESH
        )

    bufs = (buf_a, buf_b)
    pair, pair_p, pair_m, pair_2 = (pl.ds(2 * v, 2) for v in (y, yp, ym, y2))
    full = tuple((o, slice(None)) for o in range(4))
    chunks = (((0, pl.ds(0, 384)), (0, pl.ds(384, 384))) + full[1:], full)

    def ag_copy(w, k, kind, at, core, d):
        o, cols = chunks[w][k]
        b = bufs[w].at[order[o], at, core, :, cols]
        sent = ag_s.at[w, 0 if kind == 0 else 1]
        return remote(b, b, sent, ag_r.at[w, k, kind], d)

    def ag_sx(w, k):
        ag_copy(w, k, 0, own, c, d_xn).start()

    def ag_sy(w, k):
        ag_copy(w, k, 1, own, c, d_yp).start()
        ag_copy(w, k, 1, own, c, d_ym).start()

    def ag_x(w, k):
        ag_copy(w, k, 0, 2 * y + xn, c, d_xn).wait_recv()
        at = 2 * y + xn if w == 0 and k < 2 else pair
        ag_copy(w, k, 1, at, c, d_yp).start()
        ag_copy(w, k, 1, at, c, d_ym).start()
        ag_copy(w, k, 3, pair, c, d_sib).start()

    def ag_y(w, k):
        ag_copy(w, k, 1, pl.ds(0, 4), c, d_yp).wait_recv()
        ag_copy(w, k, 2, 2 * ym, c, d_yp).start()
        ag_copy(w, k, 2, 2 * yp + 1, c, d_ym).start()
        ag_copy(w, k, 3, pair_m, c, d_sib).start()
        ag_copy(w, k, 3, pair_p, c, d_sib).start()

    def ag_far(w, k):
        ag_copy(w, k, 2, pair_2, c, d_yp).wait_recv()
        ag_copy(w, k, 3, pair_2, c, d_sib).start()

    def ag_sib(w, k):
        ag_copy(w, k, 3, slice(None), cn, d_sib).wait_recv()

    def ag_drain(w):
        for i, b in enumerate((bufs[w].at[:, own, c], bufs[w].at[:, pl.ds(0, 7)])):
            remote(b, b, ag_s.at[w, i], ag_r.at[w, 0, 0], d_sib).wait_send()

    l_dout.wait()
    for o in range(4):
        buf_a[order[o], own, c] = own_dout[:, pl.ds(al(order[o] * 768, 128), 768)]
    ag_sx(0, 0)
    ag_sy(0, 0)
    ag_sx(0, 1)
    ag_sy(0, 1)
    ag_sx(0, 2)
    ag_sx(0, 3)
    ag_sx(0, 4)

    def layer_norm():
        l_tok.wait()
        l_gain.wait()
        x = own_tok[...].astype(F32)
        center = jnp.mean(x, axis=-1, keepdims=True)
        spread = jnp.mean((x - center) ** 2, axis=-1, keepdims=True)
        rstd = 1.0 / jnp.sqrt(spread + 1e-06)
        xhat[...] = (x - center) * rstd
        rstd_ref[...] = jnp.broadcast_to(rstd, rstd_ref.shape)
        for o in range(4):
            for half, dst in ((xh, buf_b.at[o, own, c, :, pl.ds(0, 384)]), (xo, nsend.at[o])):
                cols = pl.ds(al(o * 768 + half * 384, 128), 384)
                dst[...] = (xhat[:, cols] * gain[:, cols]).astype(BF16)
            nx_copy(o).start()

    def nx_copy(o):
        dst = buf_b.at[o, own, c, :, pl.ds(384, 384)]
        return remote(nsend.at[o], dst, nx_s.at[0], nx_s.at[1], d_xo)

    def nx_all():
        b = buf_b.at[:, own, c, :, pl.ds(384, 384)]
        return remote(nsend, b, nx_s.at[0], nx_s.at[1], d_xo)

    def nx_take():
        nx_all().wait_recv()
        for o in range(4):
            ag_sx(1, o)

    def att_fwd(b):
        rows = pl.ds(b * 256, 256)
        for h in range(2):
            q = qkv[rows, pl.ds(h * 128, 128)]
            k = qkv[rows, pl.ds(256 + h * 128, 128)]
            v = qkv[rows, pl.ds(512 + h * 128, 128)]
            s = nt(q, k) * SCALE
            e = jnp.exp(s - jnp.max(s, axis=-1, keepdims=True))
            p = e / jnp.sum(e, axis=-1, keepdims=True)
            pf[b * 2 + h] = p
            out = nn(p.astype(BF16), v)
            heads[rows, pl.ds(h * 128, 128)] = out.astype(BF16)
            joined_t[pl.ds(h * 128, 128), rows] = jnp.transpose(out).astype(BF16)

    def gelu(t):
        rows = pl.ds(al(t * 128, 128), 128)
        v = pre[rows, :].astype(F32)
        cumul = 0.5 * (1.0 + lax.erf(v * 0.7071067811865476))
        joined_t[pl.ds(256, 768), rows] = jnp.transpose(v * cumul).astype(BF16)
        dens = jnp.exp(-0.5 * v * v) * 0.3989422804014327
        slope[rows, :] = cumul + v * dens

    l_pre.wait()
    gelu(0)
    gelu(1)
    ag_x(0, 0)
    l_qkv.wait()
    att_fwd(0)
    ag_x(0, 1)
    att_fwd(1)
    ag_y(0, 0)
    att_fwd(2)
    ag_x(0, 2)
    gelu(2)
    ag_y(0, 1)
    ag_x(0, 3)
    layer_norm()
    gelu(3)
    gelu(4)
    gelu(5)
    ag_far(0, 0)
    ag_y(0, 2)
    ag_far(0, 1)
    ag_x(0, 4)
    ag_sib(0, 0)

    class Ring:
        def __init__(self, src, rbuf, ssem, rsem, add):
            self.src, self.rbuf, self.ssem, self.rsem, self.add = src, rbuf, ssem, rsem, add
            self.sent = []

        def send(self, i, src, d):
            cp = remote(src, self.rbuf.at[i], self.ssem.at[i], self.rsem.at[i], d)
            cp.start()
            self.sent.append(cp)

        def wait(self, i):
            b = self.rbuf.at[i]
            remote(b, b, self.ssem.at[i], self.rsem.at[i], d_zp).wait_recv()

        def far(self):
            self.send(0, self.src(z2, 1), d_zp)
            self.send(1, self.src(z2, 0), d_zm)

        def far_block(self, h):
            for i, d in ((0, d_zp), (1, d_zm)):
                cp = remote(
                    self.src(z2, 1 - i).at[h], self.rbuf.at[i, h],
                    self.ssem.at[i], self.rsem.at[i], d,
                )
                cp.start()
                if h == 0:
                    b = self.rbuf.at[i]
                    self.sent.append(remote(b, b, self.ssem.at[i], self.rsem.at[i], d))

        def near_p(self):
            self.send(2, self.src(zp, 0), d_zp)

        def near_m(self):
            self.send(3, self.src(zm, 1), d_zm)

        def relay_p(self):
            self.wait(0)
            self.add(self.rbuf.at[0], self.src(zp, 1))
            self.send(4, self.rbuf.at[0], d_zp)

        def relay_m(self):
            self.wait(1)
            self.add(self.rbuf.at[1], self.src(zm, 0))
            self.send(5, self.rbuf.at[1], d_zm)

        def arrived(self):
            for i in (2, 3, 4, 5):
                self.wait(i)

        def drain(self):
            for cp in self.sent:
                cp.wait_send()

    def adder(lead, height, tile):
        def add(dst, src):
            def step(i):
                rows = pl.ds(al(i * tile, tile), tile)
                for at in lead:
                    dst[at + (rows, slice(None))] = (
                        dst[at + (rows, slice(None))].astype(F32)
                        + src[at + (rows, slice(None))].astype(F32)
                    ).astype(BF16)

            loop(height // tile, step)

        return add

    def z_first(part, base, height):
        return lambda zz, half: part.at[pl.ds(zz * 2, 2), pl.ds(base + half * height, height), :]

    def x_first(part, base, height):
        return lambda zz, half: part.at[zz * 2 + xh, pl.ds(base + half * height, height), :]

    both = ((0,), (1,))
    ro = [
        Ring(z_first(cout, s * 2 * HO, HO), rzo.at[s], zo_s.at[s], zo_r.at[s], adder(both, HO, 48))
        for s in range(NSO)
    ]
    def in_src(n):
        return lambda zz, half: cin.at[n, zz, pl.ds(half * 192, 192), :]

    rn = [
        Ring(in_src(n), rzi.at[n], zi_s.at[n], zi_r.at[n], adder(((),), 192, 96)) for n in range(6)
    ]
    base_o = 1024 - XO
    fo = Ring(x_first(cout, base_o, XO // 2), rfo, fo_s, fo_r, adder(((),), XO // 2, 16))

    class Cross:
        def __init__(self, ring, part, rx, ssem, rsem, base, height, tile):
            self.ring, self.part, self.rx = ring, part, rx
            self.ssem, self.rsem = ssem, rsem
            self.base, self.height, self.tile = base, height, tile
            self.sent = []

        def send(self):
            self.ring.arrived()
            r = self.ring.rbuf
            for half, (a, b) in enumerate(((2, 5), (3, 4))):
                off = self.base + half * self.height

                def step(i, a=a, b=b, off=off):
                    rows = pl.ds(al(i * self.tile, self.tile), self.tile)
                    prow = pl.ds(al(off + i * self.tile, self.tile), self.tile)
                    r[a, xo, rows, :] = (
                        r[a, xo, rows, :].astype(F32)
                        + r[b, xo, rows, :].astype(F32)
                        + self.part[z * 2 + xo, prow, :].astype(F32)
                    ).astype(BF16)

                loop(self.height // self.tile, step)
                cp = remote(
                    r.at[a, xo], self.rx.at[pl.ds(off, self.height), :],
                    self.ssem.at[half], self.rsem.at[half], d_xo,
                )
                cp.start()
                self.sent.append(cp)

        def finish(self):
            r = self.ring.rbuf
            for half, (a, b) in enumerate(((2, 5), (3, 4))):
                off = self.base + half * self.height
                dst = self.rx.at[pl.ds(off, self.height), :]
                remote(dst, dst, self.ssem.at[half], self.rsem.at[half], d_xo).wait_recv()

                def step(i, a=a, b=b, off=off):
                    rows = pl.ds(al(i * self.tile, self.tile), self.tile)
                    prow = pl.ds(al(off + i * self.tile, self.tile), self.tile)
                    self.rx[prow, :] = (
                        r[a, xh, rows, :].astype(F32)
                        + r[b, xh, rows, :].astype(F32)
                        + self.part[z * 2 + xh, prow, :].astype(F32)
                        + self.rx[prow, :].astype(F32)
                    ).astype(BF16)

                loop(self.height // self.tile, step)

        def drain(self):
            for cp in self.sent:
                cp.wait_send()

    class First:
        def __init__(self, ring, part, x1, rx, ssem, rsem, base, height, tile):
            self.ring, self.part, self.x1, self.rx = ring, part, x1, rx
            self.ssem, self.rsem = ssem, rsem
            self.base, self.height, self.tile = base, height, tile

        def copy(self, o):
            return remote(
                self.part.at[order[o] * 2 + xo, pl.ds(self.base, self.height), :],
                self.x1.at[o], self.ssem.at[o], self.rsem.at[o], d_xo,
            )

        def send(self, o):
            self.copy(o).start()

        def take(self, o):
            self.copy(o).wait_recv()

            def step(i):
                rows = pl.ds(al(i * self.tile, self.tile), self.tile)
                prow = pl.ds(al(self.base + i * self.tile, self.tile), self.tile)
                mine = order[o] * 2 + xh
                self.part[mine, prow, :] = (
                    self.part[mine, prow, :].astype(F32) + self.x1[o, rows, :].astype(F32)
                ).astype(BF16)

            loop(self.height // self.tile, step)
            if o < 3:
                (self.ring.far, self.ring.near_p, self.ring.near_m)[o]()

        def finish(self):
            self.ring.arrived()
            r = self.ring.rbuf
            half_rows = self.height // 2
            for half, (a, b) in enumerate(((2, 5), (3, 4))):
                off = self.base + half * half_rows

                def step(i, a=a, b=b, off=off):
                    rows = pl.ds(al(i * self.tile, self.tile), self.tile)
                    prow = pl.ds(al(off + i * self.tile, self.tile), self.tile)
                    self.rx[prow, :] = (
                        r[a, rows, :].astype(F32)
                        + r[b, rows, :].astype(F32)
                        + self.part[z * 2 + xh, prow, :].astype(F32)
                    ).astype(BF16)

                loop(half_rows // self.tile, step)

        def drain(self):
            for o in range(4):
                self.copy(o).wait_send()

    co = [
        Cross(ro[s], cout, rxo, xo_s.at[s], xo_r.at[s], s * 2 * HO, HO, 48) for s in range(NSO)
    ]
    xfo = First(fo, cout, x1o, rxo, x1o_s, x1o_r, base_o, XO, 16)

    def out_half(h):
        j = order[0]

        def step(r):
            rows = pl.ds(al(r * 256, 256), 256)
            right_side = buf_a[j, :, :, :, pl.ds(h * 384, 384)].reshape(768, 384)
            cout[j * 2 + h, rows, :] = nn(joined_t[rows, :], right_side).astype(BF16)

        loop(4, step)

    def out_chunk(o):
        j = order[o]

        def step(r):
            rows = pl.ds(al(r * 256, 256), 256)
            t = nn(joined_t[rows, :], buf_a[j].reshape(768, 768)).astype(BF16)
            cout[j * 2, rows, :] = t[:, :384]
            cout[j * 2 + 1, rows, :] = t[:, 384:]

        loop(4, step)

    out_half(0)
    for r in ro:
        r.far_block(0)
    nx_take()
    ag_sib(0, 1)
    out_half(1)
    for r in ro:
        r.far_block(1)
    xfo.send(0)
    ag_far(0, 2)
    ag_y(0, 3)
    ag_sib(0, 2)
    out_chunk(1)
    for r in ro:
        r.near_p()
    xfo.send(1)
    ag_far(0, 3)
    ag_y(0, 4)
    ag_x(1, 0)
    ag_sib(0, 3)
    out_chunk(2)
    for r in ro:
        r.near_m()
    xfo.send(2)
    ag_far(0, 4)
    ag_x(1, 1)
    ag_sib(0, 4)
    ag_y(1, 0)

    def joined_grad(nb):
        for l in wo_loads[nb]:
            l.wait()
        row = wo_rows[nb]

        def step(r):
            rows = pl.ds(al(r * 384, 128), 384)
            acc = jnp.zeros((384, 256), F32)
            for j in range(4):
                w = wslot[pl.ds(row + (j // 2) * 256, 256), pl.ds((j % 2) * 768, 768)]
                acc = acc + nt(buf_a[j, pl.ds(r * 4, 4)].reshape(384, 768), w)
            g = acc.astype(BF16)
            if nb == 0:
                gh[rows, :] = g
            else:
                cols = pl.ds((nb - 1) * 256, 256)
                gproj[2 + nb, rows, :] = (g.astype(F32) * slope[rows, cols]).astype(BF16)

        loop(2, step)

    def gx_copy(n):
        return remote(gproj.at[n], gp2.at[n], gx_s, gx_r.at[n], d_xo)

    def gx_send(n):
        gx_copy(n).start()

    def gx_wait(n):
        gx_copy(n).wait_recv()

    joined_grad(1)
    gx_send(3)
    for l in wo_loads[0]:
        l.start()
    ag_x(1, 2)
    ag_y(1, 1)
    out_chunk(3)
    xfo.send(3)
    ag_x(1, 3)
    ag_far(1, 0)
    ro[0].relay_p()
    ro[0].relay_m()
    joined_grad(2)
    gx_send(4)
    ag_far(1, 1)
    ag_y(1, 2)
    xfo.take(0)
    joined_grad(3)
    gx_send(5)
    ro[1].relay_p()
    ro[1].relay_m()
    ag_far(1, 2)
    ag_y(1, 3)
    joined_grad(0)
    ro[2].relay_p()
    ro[2].relay_m()

    def win_load(j):
        return load(
            win.at[pl.ds(j * 768, 768), :], wslot.at[pl.ds((j % 2) * 768, 768)], 4 + j
        )

    win_load(0).start()
    win_load(1).start()

    def att_bwd(b):
        rows = pl.ds(b * 256, 256)
        for h in range(2):
            q = qkv[rows, pl.ds(h * 128, 128)]
            k = qkv[rows, pl.ds(256 + h * 128, 128)]
            v = qkv[rows, pl.ds(512 + h * 128, 128)]
            g = gh[rows, pl.ds(h * 128, 128)]
            p = pf[b * 2 + h]
            delta = jnp.sum(
                g.astype(F32) * heads[rows, pl.ds(h * 128, 128)].astype(F32),
                axis=-1, keepdims=True,
            )
            ds = (p * (nt(g, v) - delta) * SCALE).astype(BF16)
            gproj[2, rows, pl.ds(h * 128, 128)] = tn(p.astype(BF16), g).astype(BF16)
            gproj[0, rows, pl.ds(h * 128, 128)] = nn(ds, k).astype(BF16)
            gproj[1, rows, pl.ds(h * 128, 128)] = tn(ds, q).astype(BF16)

    att_bwd(0)
    att_bwd(1)
    att_bwd(2)
    gx_send(2)
    gx_send(0)
    gx_send(1)
    ag_far(1, 3)
    xfo.take(1)

    ag_drain(0)

    def transposed(o):
        ag_sib(1, o)
        j = order[o]

        def step(i):
            block = buf_b[j, pl.ds(i * 4, 4)].reshape(384, 768)
            rows = pl.ds(al(i * 384, 128), 384)
            buf_a[j, :, :, :, rows] = jnp.transpose(block).reshape(8, 2, 48, 384)

        loop(2, step)

    def in_block(n, o):
        j = order[o]
        left_own = buf_a[j, pl.ds(0, 4)].reshape(384, 768)
        left_other = buf_a[j, pl.ds(4, 4)].reshape(384, 768)
        cin[n, j] = (nn(left_own, gproj[n]) + nn(left_other, gp2[n])).astype(BF16)

    def in_finish(n):
        rn[n].arrived()
        r = rzi.at[n]
        for half, (a, b) in enumerate(((2, 5), (3, 4))):
            rows = pl.ds(half * 192, 192)
            rxi[n, rows, :] = (
                r[a].astype(F32) + r[b].astype(F32) + cin[n, z, rows, :].astype(F32)
            ).astype(BF16)

    transposed(0)
    transposed(1)
    transposed(2)
    transposed(3)
    ag_drain(1)
    gx_wait(3)
    in_block(3, 0)
    rn[3].far()
    in_block(3, 1)
    rn[3].near_p()
    in_block(3, 2)
    rn[3].near_m()
    in_block(3, 3)
    xfo.take(2)
    xfo.take(3)

    def sib_copy(j):
        return remote(buf_b.at[j, :, cn], rs_sib.at[j], m_s.at[0], ms_r.at[j], d_sib)

    def normed_grad(j):
        win_load(j).wait()
        base = (j % 2) * 768

        def step(i):
            h, n = i // 3, i % 3
            rows = pl.ds(al(h * 384, 128), 384)
            w = wslot[pl.ds(al(base + n * 256, 256), 256), :]
            acc = nt(gproj[0, rows, :], w[:, :256])
            for k in range(1, 6):
                acc = acc + nt(gproj[k, rows, :], w[:, k * 256 : k * 256 + 256])
            t = acc.astype(BF16)
            cols = pl.ds(al(n * 256, 128), 256)
            buf_b[j, pl.ds(h * 4, 4), :, :, cols] = t.reshape(4, 2, 48, 256)

        loop(6, step)
        sib_copy(j).start()
        if j < 2:
            win_load(j + 2).start()

    y_out = ((pair_p, d_yp), (pair_m, d_ym), (pair_2, d_y2))

    def sib_sum(j):
        sib_copy(j).wait_recv()

        def step(i):
            buf_b[j, i, c] = (buf_b[j, i, c].astype(F32) + rs_sib[j, i].astype(F32)).astype(BF16)

        loop(8, step)
        for i, (at, d) in enumerate(y_out):
            remote(buf_b.at[j, at, c], rs_y.at[j, i], m_s.at[1], my_r.at[j], d).start()

    def x_copy(j):
        return remote(ss_x.at[j], rs_x.at[j], m_s.at[2], mx_r.at[j], d_xn)

    def y_sum(j):
        remote(rs_y.at[j], rs_y.at[j], m_s.at[1], my_r.at[j], d_yp).wait_recv()

        def total(side):
            acc = buf_b[j, 2 * y + side, c].astype(F32)
            for i in range(3):
                acc = acc + rs_y[j, i, side].astype(F32)
            return acc

        ss_x[j] = total(xn).astype(BF16)
        x_copy(j).start()
        gn[:, pl.ds(j * 768, 768)] = total(xl)

    def x_sum(j):
        x_copy(j).wait_recv()
        cols = pl.ds(j * 768, 768)
        gn[:, cols] = gn[:, cols] + rs_x[j].astype(F32)

    normed_grad(0)
    gx_wait(4)
    in_block(4, 0)
    rn[4].far()
    in_block(4, 1)
    rn[4].near_p()
    in_block(4, 2)
    rn[4].near_m()
    in_block(4, 3)
    normed_grad(1)
    sib_sum(0)
    fo.relay_p()
    fo.relay_m()
    gx_wait(5)
    in_block(5, 0)
    rn[5].far()
    in_block(5, 1)
    rn[5].near_p()
    in_block(5, 2)
    rn[5].near_m()
    in_block(5, 3)
    rn[3].relay_p()
    rn[3].relay_m()
    normed_grad(2)
    sib_sum(1)
    rn[4].relay_p()
    rn[4].relay_m()
    co[0].send()
    co[1].send()
    gx_wait(2)
    in_block(2, 0)
    rn[2].far()
    in_block(2, 1)
    rn[2].near_p()
    in_block(2, 2)
    rn[2].near_m()
    in_block(2, 3)
    normed_grad(3)
    sib_sum(2)
    y_sum(0)
    rn[5].relay_p()
    rn[5].relay_m()
    co[2].send()
    gx_wait(0)
    in_block(0, 0)
    rn[0].far()
    in_block(0, 1)
    rn[0].near_p()
    in_block(0, 2)
    rn[0].near_m()
    in_block(0, 3)
    sib_sum(3)
    y_sum(1)
    rn[2].relay_p()
    rn[2].relay_m()
    in_finish(3)
    in_finish(4)
    xfo.finish()
    gx_wait(1)
    in_block(1, 0)
    rn[1].far()
    in_block(1, 1)
    rn[1].near_p()
    in_block(1, 2)
    rn[1].near_m()
    in_block(1, 3)
    rn[0].relay_p()
    rn[0].relay_m()
    y_sum(2)
    y_sum(3)
    in_finish(5)
    rn[1].relay_p()
    rn[1].relay_m()
    in_finish(2)
    in_finish(0)
    co[0].finish()
    co[1].finish()
    co[2].finish()
    st_o = load(rxo, gwout, 1)
    st_o.start()
    in_finish(1)
    for j in range(4):
        x_sum(j)
    xh_v = xhat[...]
    sg = gn[...] * gain[...]
    m1 = jnp.mean(sg, axis=-1, keepdims=True)
    m2 = jnp.mean(sg * xh_v, axis=-1, keepdims=True)
    own_tok[...] = (
        own_dout[...].astype(F32) + (sg - m1 - xh_v * m2) * rstd_ref[:, :1]
    ).astype(BF16)
    st_g = load(own_tok, ig, 0)
    st_g.start()
    st_i = [load(rxi.at[n], gwin.at[:, pl.ds(n * 256, 256)], 2 + n) for n in range(6)]
    for st in st_i:
        st.start()
    gx_all = remote(gproj, gp2, gx_s, gx_r.at[0], d_xo)
    gx_all.wait_send()
    nx_all().wait_send()
    for r in ro + rn + [fo] + co + [xfo]:
        r.drain()
    for b, i in ((rs_sib, 0), (rs_y, 1), (rs_x, 2)):
        remote(b, b, m_s.at[i], mx_r.at[0], d_sib).wait_send()
    st_o.wait()
    st_g.wait()
    for st in st_i:
        st.wait()


def widen(ig, gwin, gwout, ig_out, gwin_out, gwout_out, tg, ti, to, fi, fo, isem, osem):
    def copies(k):
        if k == 8:
            return ig, tg, tg, ig_out
        if k < 4:
            at = pl.ds(k * 96, 96)
            return gwin.at[at], ti.at[at], fi.at[at], gwin_out.at[at]
        at = pl.ds((k - 4) * 256, 256)
        return gwout.at[at], to.at[at], fo.at[at], gwout_out.at[at]

    ins = [pltpu.make_async_copy(copies(k)[0], copies(k)[1], isem.at[k]) for k in range(9)]
    outs = [pltpu.make_async_copy(copies(k)[2], copies(k)[3], osem.at[k]) for k in range(9)]
    for cp in ins:
        cp.start()
    for k in range(9):
        ins[k].wait()
        if k < 8:
            src, dst = copies(k)[1:3]
            dst[...] = src[...].astype(F32)
        outs[k].start()
    for cp in outs:
        cp.wait()


def body(block_input_tokens, norm_gain_vector, w_in, w_out, saved_qkv, mlp_pre, output_gradient):
    hbm = pl.BlockSpec(memory_space=pl.ANY)
    sem = pltpu.SemaphoreType.DMA
    v = pltpu.VMEM
    ig, gwin, gwout = pl.pallas_call(
        kernel,
        name="block_backward",
        out_shape=(
            jax.ShapeDtypeStruct((48, 3072), BF16),
            jax.ShapeDtypeStruct((384, 1536), BF16),
            jax.ShapeDtypeStruct((1024, 384), BF16),
        ),
        in_specs=[hbm] * 7,
        out_specs=(hbm, hbm, hbm),
        scratch_shapes=[
            v((4, 8, 2, 48, 768), BF16), v((4, 8, 2, 48, 768), BF16), v((768, 768), BF16),
            v((768, 768), BF16), v((768, 768), F32), v((6, 256, 256), F32),
            v((768, 256), BF16), v((1024, 768), BF16), v((768, 256), BF16),
            v((6, 768, 256), BF16), v((6, 768, 256), BF16), v((1536, 1536), BF16),
            v((8, 1024, 384), BF16), v((6, 4, 384, 256), BF16),
            v((NSO, 6, 2, HO, 384), BF16), v((6, 6, 192, 256), BF16),
            v((6, XO // 2, 384), BF16), v((4, XO, 384), BF16),
            v((1024, 384), BF16), v((6, 384, 256), BF16), v((4, 48, 384), BF16),
            v((4, 8, 48, 768), BF16),
            v((4, 3, 2, 48, 768), BF16), v((4, 48, 768), BF16), v((4, 48, 768), BF16),
            v((48, 3072), F32), v((48, 3072), F32), v((1, 3072), F32), v((48, 3072), BF16),
            v((48, 3072), BF16), v((48, 128), F32),
            sem((16,)), sem((2, 2)), sem((2, 5, 4)),
            sem((NSO, 6)), sem((NSO, 6)), sem((6, 6)), sem((6, 6)), sem((6,)), sem((6,)),
            sem((NSO, 2)), sem((NSO, 2)),
            sem((4,)), sem((4,)), sem, sem((6,)), sem((2,)), sem((3,)), sem((4,)), sem((4,)), sem((4,)),
        ],
        compiler_params=pltpu.CompilerParams(
            collective_id=0, has_side_effects=True, vmem_limit_bytes=63 << 20
        ),
    )(
        block_input_tokens, norm_gain_vector.reshape(1, -1), w_in, w_out, saved_qkv, mlp_pre,
        output_gradient,
    )
    return pl.pallas_call(
        widen,
        name="widen",
        out_shape=(
            jax.ShapeDtypeStruct((48, 3072), BF16),
            jax.ShapeDtypeStruct((384, 1536), F32),
            jax.ShapeDtypeStruct((1024, 384), F32),
        ),
        in_specs=[hbm] * 3,
        out_specs=(hbm,) * 3,
        scratch_shapes=[
            v((48, 3072), BF16), v((384, 1536), BF16), v((1024, 384), BF16),
            v((384, 1536), F32), v((1024, 384), F32), sem((9,)), sem((9,)),
        ],
        compiler_params=pltpu.CompilerParams(vmem_limit_bytes=62 << 20),
    )(ig, gwin, gwout)


def solution(mesh):
    placed = (
        P(("dp", "mp"), None),
        P(),
        P(None, "mp"),
        P("mp", None),
        P("dp", "mp"),
        P("dp", "mp"),
        P(("dp", "mp"), None),
    )
    return jax.shard_map(
        body,
        mesh=mesh,
        in_specs=placed,
        out_specs=(P(("dp", "mp"), None), P("dp", "mp"), P("mp", "dp")),
        check_vma=False,
    )
```

```python
import functools

import jax
import jax.numpy as jnp
from jax import lax
from jax.experimental import pallas as pl
from jax.experimental.pallas import tpu as pltpu
from jax.sharding import PartitionSpec as P

HD = 128
F32 = jnp.float32
BF16 = jnp.bfloat16
SCALE = HD ** (-0.5)
MESH = pl.DeviceIdType.MESH
NSO, HO, XO = 3, 144, 160
BLOCKS = (3, 4, 5, 2, 0, 1)


def nt(a, b):
    return lax.dot_general(a, b, (((1,), (1,)), ((), ())), preferred_element_type=F32)


def nn(a, b):
    return lax.dot_general(a, b, (((1,), (0,)), ((), ())), preferred_element_type=F32)


def tn(a, b):
    return lax.dot_general(a, b, (((0,), (0,)), ((), ())), preferred_element_type=F32)


def loop(n, fn):
    def step(i, carry):
        fn(i)
        return carry

    if n == 1:
        fn(0)
    else:
        lax.fori_loop(0, n, step, 0)


def al(v, m):
    return pl.multiple_of(v, m)


def kernel(
    tok, gain_hbm, win, wout, qkv_hbm, pre_hbm, dout,
    ig, gwin, gwout,
    buf_a, buf_b, qkv, pre, slope, pf, heads, joined_t, gh, gproj, gp2, wslot, cout, cin,
    rzo, rzi, rfo, x1o, rxo, rxi, nsend, rs_sib, rs_y, rs_x, ss_x, xhat, gn, gain,
    own_tok, own_dout, rstd_ref,
    lsem, ag_s, ag_r, zo_s, zo_r, zi_s, zi_r, fo_s, fo_r, xo_s, xo_r,
    x1o_s, x1o_r, gx_s, gx_r, nx_s, m_s, ms_r, my_r, mx_r,
):
    dp = lax.axis_index("dp")
    mp = lax.axis_index("mp")
    z = dp // 2
    xh = dp % 2
    y = mp // 4
    xl = (mp // 2) % 2
    c = mp % 2
    zp, zm, z2 = (z + 1) % 4, (z + 3) % 4, (z + 2) % 4
    yp, ym, y2 = (y + 1) % 4, (y + 3) % 4, (y + 2) % 4
    xn, cn, xo = 1 - xl, 1 - c, 1 - xh

    def m_of(yy, xx, cc):
        return yy * 4 + xx * 2 + cc

    d_sib = (dp, m_of(y, xl, cn))
    d_xn = (dp, m_of(y, xn, c))
    d_yp = (dp, m_of(yp, xl, c))
    d_ym = (dp, m_of(ym, xl, c))
    d_y2 = (dp, m_of(y2, xl, c))
    d_zp = (zp * 2 + xh, mp)
    d_zm = (zm * 2 + xh, mp)
    d_xo = (z * 2 + xo, mp)
    friends = (d_sib, d_xn, d_yp, d_ym, d_y2, d_zp, d_zm, d_xo)

    def load(src, dst, i):
        return pltpu.make_async_copy(src, dst, lsem.at[i])

    own = 2 * y + xl
    order = (z2, zp, zm, z)
    l_dout = load(dout, own_dout, 12)
    l_tok = load(tok, own_tok, 0)
    l_gain = load(gain_hbm, gain, 1)
    l_qkv = load(qkv_hbm, qkv, 2)
    l_pre = load(pre_hbm, pre, 3)
    for l in (l_dout, l_tok, l_gain, l_qkv, l_pre):
        l.start()

    def wout_loads(nb, row):
        return [
            load(
                wout.at[pl.ds(nb * 256, 256), pl.ds(h * 1536, 1536)],
                wslot.at[pl.ds(row + h * 256, 256)],
                4 + nb * 2 + h,
            )
            for h in range(2)
        ]

    wo_rows = (0, 0, 512, 1024)
    wo_loads = [wout_loads(nb, wo_rows[nb]) for nb in range(4)]
    for nb in range(1, 4):
        for l in wo_loads[nb]:
            l.start()

    barrier = pltpu.get_barrier_semaphore()
    for d in friends:
        pl.semaphore_signal(barrier, inc=1, device_id=d, device_id_type=MESH)
    pl.semaphore_wait(barrier, len(friends))

    def remote(src, dst, s, r, d):
        return pltpu.make_async_remote_copy(
            src_ref=src, dst_ref=dst, send_sem=s, recv_sem=r, device_id=d, device_id_type=MESH
        )

    bufs = (buf_a, buf_b)
    pair, pair_p, pair_m, pair_2 = (pl.ds(2 * v, 2) for v in (y, yp, ym, y2))
    full = tuple((o, slice(None)) for o in range(4))
    chunks = (((0, pl.ds(0, 384)), (0, pl.ds(384, 384))) + full[1:], full)

    def ag_copy(w, k, kind, at, core, d):
        o, cols = chunks[w][k]
        b = bufs[w].at[order[o], at, core, :, cols]
        sent = ag_s.at[w, 0 if kind == 0 else 1]
        return remote(b, b, sent, ag_r.at[w, k, kind], d)

    def ag_sx(w, k):
        ag_copy(w, k, 0, own, c, d_xn).start()

    def ag_sy(w, k):
        ag_copy(w, k, 1, own, c, d_yp).start()
        ag_copy(w, k, 1, own, c, d_ym).start()

    def ag_x(w, k):
        ag_copy(w, k, 0, 2 * y + xn, c, d_xn).wait_recv()
        at = 2 * y + xn if w == 0 and k < 2 else pair
        ag_copy(w, k, 1, at, c, d_yp).start()
        ag_copy(w, k, 1, at, c, d_ym).start()
        ag_copy(w, k, 3, pair, c, d_sib).start()

    def ag_y(w, k):
        ag_copy(w, k, 1, pl.ds(0, 4), c, d_yp).wait_recv()
        ag_copy(w, k, 2, 2 * ym, c, d_yp).start()
        ag_copy(w, k, 2, 2 * yp + 1, c, d_ym).start()
        ag_copy(w, k, 3, pair_m, c, d_sib).start()
        ag_copy(w, k, 3, pair_p, c, d_sib).start()

    def ag_far(w, k):
        ag_copy(w, k, 2, pair_2, c, d_yp).wait_recv()
        ag_copy(w, k, 3, pair_2, c, d_sib).start()

    def ag_sib(w, k):
        ag_copy(w, k, 3, slice(None), cn, d_sib).wait_recv()

    def ag_drain(w):
        for i, b in enumerate((bufs[w].at[:, own, c], bufs[w].at[:, pl.ds(0, 7)])):
            remote(b, b, ag_s.at[w, i], ag_r.at[w, 0, 0], d_sib).wait_send()

    l_dout.wait()
    for o in range(4):
        buf_a[order[o], own, c] = own_dout[:, pl.ds(al(order[o] * 768, 128), 768)]
    ag_sx(0, 0)
    ag_sy(0, 0)
    ag_sx(0, 1)
    ag_sy(0, 1)
    ag_sx(0, 2)
    ag_sx(0, 3)
    ag_sx(0, 4)

    def layer_norm():
        l_tok.wait()
        l_gain.wait()
        x = own_tok[...].astype(F32)
        center = jnp.mean(x, axis=-1, keepdims=True)
        spread = jnp.mean((x - center) ** 2, axis=-1, keepdims=True)
        rstd = 1.0 / jnp.sqrt(spread + 1e-06)
        xhat[...] = (x - center) * rstd
        rstd_ref[...] = jnp.broadcast_to(rstd, rstd_ref.shape)
        for o in range(4):
            for half, dst in ((xh, buf_b.at[o, own, c, :, pl.ds(0, 384)]), (xo, nsend.at[o])):
                cols = pl.ds(al(o * 768 + half * 384, 128), 384)
                dst[...] = (xhat[:, cols] * gain[:, cols]).astype(BF16)
            nx_copy(o).start()

    def nx_copy(o):
        dst = buf_b.at[o, own, c, :, pl.ds(384, 384)]
        return remote(nsend.at[o], dst, nx_s.at[0], nx_s.at[1], d_xo)

    def nx_all():
        b = buf_b.at[:, own, c, :, pl.ds(384, 384)]
        return remote(nsend, b, nx_s.at[0], nx_s.at[1], d_xo)

    def nx_take():
        nx_all().wait_recv()
        for o in range(4):
            ag_sx(1, o)

    def att_fwd(b):
        rows = pl.ds(b * 256, 256)
        for h in range(2):
            q = qkv[rows, pl.ds(h * 128, 128)]
            k = qkv[rows, pl.ds(256 + h * 128, 128)]
            v = qkv[rows, pl.ds(512 + h * 128, 128)]
            s = nt(q, k) * SCALE
            e = jnp.exp(s - jnp.max(s, axis=-1, keepdims=True))
            p = e / jnp.sum(e, axis=-1, keepdims=True)
            pf[b * 2 + h] = p
            out = nn(p.astype(BF16), v)
            heads[rows, pl.ds(h * 128, 128)] = out.astype(BF16)
            joined_t[pl.ds(h * 128, 128), rows] = jnp.transpose(out).astype(BF16)

    def gelu(t):
        rows = pl.ds(al(t * 128, 128), 128)
        v = pre[rows, :].astype(F32)
        cumul = 0.5 * (1.0 + lax.erf(v * 0.7071067811865476))
        joined_t[pl.ds(256, 768), rows] = jnp.transpose(v * cumul).astype(BF16)
        dens = jnp.exp(-0.5 * v * v) * 0.3989422804014327
        slope[rows, :] = cumul + v * dens

    l_pre.wait()
    gelu(0)
    gelu(1)
    ag_x(0, 0)
    l_qkv.wait()
    att_fwd(0)
    ag_x(0, 1)
    att_fwd(1)
    ag_y(0, 0)
    att_fwd(2)
    ag_x(0, 2)
    gelu(2)
    ag_y(0, 1)
    ag_x(0, 3)
    layer_norm()
    gelu(3)
    gelu(4)
    gelu(5)
    ag_far(0, 0)
    ag_y(0, 2)
    ag_far(0, 1)
    ag_x(0, 4)
    ag_sib(0, 0)

    class Ring:
        def __init__(self, src, rbuf, ssem, rsem, add):
            self.src, self.rbuf, self.ssem, self.rsem, self.add = src, rbuf, ssem, rsem, add
            self.sent = []

        def send(self, i, src, d):
            cp = remote(src, self.rbuf.at[i], self.ssem.at[i], self.rsem.at[i], d)
            cp.start()
            self.sent.append(cp)

        def wait(self, i):
            b = self.rbuf.at[i]
            remote(b, b, self.ssem.at[i], self.rsem.at[i], d_zp).wait_recv()

        def far(self):
            self.send(0, self.src(z2, 1), d_zp)
            self.send(1, self.src(z2, 0), d_zm)

        def far_block(self, h):
            for i, d in ((0, d_zp), (1, d_zm)):
                cp = remote(
                    self.src(z2, 1 - i).at[h], self.rbuf.at[i, h],
                    self.ssem.at[i], self.rsem.at[i], d,
                )
                cp.start()
                if h == 0:
                    b = self.rbuf.at[i]
                    self.sent.append(remote(b, b, self.ssem.at[i], self.rsem.at[i], d))

        def near_p(self):
            self.send(2, self.src(zp, 0), d_zp)

        def near_m(self):
            self.send(3, self.src(zm, 1), d_zm)

        def relay_p(self):
            self.wait(0)
            self.add(self.rbuf.at[0], self.src(zp, 1))
            self.send(4, self.rbuf.at[0], d_zp)

        def relay_m(self):
            self.wait(1)
            self.add(self.rbuf.at[1], self.src(zm, 0))
            self.send(5, self.rbuf.at[1], d_zm)

        def arrived(self):
            for i in (2, 3, 4, 5):
                self.wait(i)

        def drain(self):
            for cp in self.sent:
                cp.wait_send()

    def adder(lead, height, tile):
        def add(dst, src):
            def step(i):
                rows = pl.ds(al(i * tile, tile), tile)
                for at in lead:
                    dst[at + (rows, slice(None))] = (
                        dst[at + (rows, slice(None))].astype(F32)
                        + src[at + (rows, slice(None))].astype(F32)
                    ).astype(BF16)

            loop(height // tile, step)

        return add

    def z_first(part, base, height):
        return lambda zz, half: part.at[pl.ds(zz * 2, 2), pl.ds(base + half * height, height), :]

    def x_first(part, base, height):
        return lambda zz, half: part.at[zz * 2 + xh, pl.ds(base + half * height, height), :]

    both = ((0,), (1,))
    ro = [
        Ring(z_first(cout, s * 2 * HO, HO), rzo.at[s], zo_s.at[s], zo_r.at[s], adder(both, HO, 48))
        for s in range(NSO)
    ]
    def in_src(n):
        return lambda zz, half: cin.at[n, zz, pl.ds(half * 192, 192), :]

    rn = [
        Ring(in_src(n), rzi.at[n], zi_s.at[n], zi_r.at[n], adder(((),), 192, 96)) for n in range(6)
    ]
    base_o = 1024 - XO
    fo = Ring(x_first(cout, base_o, XO // 2), rfo, fo_s, fo_r, adder(((),), XO // 2, 16))

    class Cross:
        def __init__(self, ring, part, rx, ssem, rsem, base, height, tile):
            self.ring, self.part, self.rx = ring, part, rx
            self.ssem, self.rsem = ssem, rsem
            self.base, self.height, self.tile = base, height, tile
            self.sent = []

        def send(self):
            self.ring.arrived()
            r = self.ring.rbuf
            for half, (a, b) in enumerate(((2, 5), (3, 4))):
                off = self.base + half * self.height

                def step(i, a=a, b=b, off=off):
                    rows = pl.ds(al(i * self.tile, self.tile), self.tile)
                    prow = pl.ds(al(off + i * self.tile, self.tile), self.tile)
                    r[a, xo, rows, :] = (
                        r[a, xo, rows, :].astype(F32)
                        + r[b, xo, rows, :].astype(F32)
                        + self.part[z * 2 + xo, prow, :].astype(F32)
                    ).astype(BF16)

                loop(self.height // self.tile, step)
                cp = remote(
                    r.at[a, xo], self.rx.at[pl.ds(off, self.height), :],
                    self.ssem.at[half], self.rsem.at[half], d_xo,
                )
                cp.start()
                self.sent.append(cp)

        def finish(self):
            r = self.ring.rbuf
            for half, (a, b) in enumerate(((2, 5), (3, 4))):
                off = self.base + half * self.height
                dst = self.rx.at[pl.ds(off, self.height), :]
                remote(dst, dst, self.ssem.at[half], self.rsem.at[half], d_xo).wait_recv()

                def step(i, a=a, b=b, off=off):
                    rows = pl.ds(al(i * self.tile, self.tile), self.tile)
                    prow = pl.ds(al(off + i * self.tile, self.tile), self.tile)
                    self.rx[prow, :] = (
                        r[a, xh, rows, :].astype(F32)
                        + r[b, xh, rows, :].astype(F32)
                        + self.part[z * 2 + xh, prow, :].astype(F32)
                        + self.rx[prow, :].astype(F32)
                    ).astype(BF16)

                loop(self.height // self.tile, step)

        def drain(self):
            for cp in self.sent:
                cp.wait_send()

    class First:
        def __init__(self, ring, part, x1, rx, ssem, rsem, base, height, tile):
            self.ring, self.part, self.x1, self.rx = ring, part, x1, rx
            self.ssem, self.rsem = ssem, rsem
            self.base, self.height, self.tile = base, height, tile

        def copy(self, o):
            return remote(
                self.part.at[order[o] * 2 + xo, pl.ds(self.base, self.height), :],
                self.x1.at[o], self.ssem.at[o], self.rsem.at[o], d_xo,
            )

        def send(self, o):
            self.copy(o).start()

        def take(self, o):
            self.copy(o).wait_recv()

            def step(i):
                rows = pl.ds(al(i * self.tile, self.tile), self.tile)
                prow = pl.ds(al(self.base + i * self.tile, self.tile), self.tile)
                mine = order[o] * 2 + xh
                self.part[mine, prow, :] = (
                    self.part[mine, prow, :].astype(F32) + self.x1[o, rows, :].astype(F32)
                ).astype(BF16)

            loop(self.height // self.tile, step)
            if o < 3:
                (self.ring.far, self.ring.near_p, self.ring.near_m)[o]()

        def finish(self):
            self.ring.arrived()
            r = self.ring.rbuf
            half_rows = self.height // 2
            for half, (a, b) in enumerate(((2, 5), (3, 4))):
                off = self.base + half * half_rows

                def step(i, a=a, b=b, off=off):
                    rows = pl.ds(al(i * self.tile, self.tile), self.tile)
                    prow = pl.ds(al(off + i * self.tile, self.tile), self.tile)
                    self.rx[prow, :] = (
                        r[a, rows, :].astype(F32)
                        + r[b, rows, :].astype(F32)
                        + self.part[z * 2 + xh, prow, :].astype(F32)
                    ).astype(BF16)

                loop(half_rows // self.tile, step)

        def drain(self):
            for o in range(4):
                self.copy(o).wait_send()

    co = [
        Cross(ro[s], cout, rxo, xo_s.at[s], xo_r.at[s], s * 2 * HO, HO, 48) for s in range(NSO)
    ]
    xfo = First(fo, cout, x1o, rxo, x1o_s, x1o_r, base_o, XO, 16)

    def out_half(h):
        j = order[0]

        def step(r):
            rows = pl.ds(al(r * 256, 256), 256)
            right_side = buf_a[j, :, :, :, pl.ds(h * 384, 384)].reshape(768, 384)
            cout[j * 2 + h, rows, :] = nn(joined_t[rows, :], right_side).astype(BF16)

        loop(4, step)

    def out_chunk(o):
        j = order[o]

        def step(r):
            rows = pl.ds(al(r * 256, 256), 256)
            t = nn(joined_t[rows, :], buf_a[j].reshape(768, 768)).astype(BF16)
            cout[j * 2, rows, :] = t[:, :384]
            cout[j * 2 + 1, rows, :] = t[:, 384:]

        loop(4, step)

    out_half(0)
    for r in ro:
        r.far_block(0)
    nx_take()
    ag_sib(0, 1)
    out_half(1)
    for r in ro:
        r.far_block(1)
    xfo.send(0)
    ag_far(0, 2)
    ag_y(0, 3)
    ag_sib(0, 2)
    out_chunk(1)
    for r in ro:
        r.near_p()
    xfo.send(1)
    ag_far(0, 3)
    ag_y(0, 4)
    ag_x(1, 0)
    ag_sib(0, 3)
    out_chunk(2)
    for r in ro:
        r.near_m()
    xfo.send(2)
    ag_far(0, 4)
    ag_x(1, 1)
    ag_sib(0, 4)
    ag_y(1, 0)

    def joined_grad(nb):
        for l in wo_loads[nb]:
            l.wait()
        row = wo_rows[nb]

        def step(r):
            rows = pl.ds(al(r * 384, 128), 384)
            acc = jnp.zeros((384, 256), F32)
            for j in range(4):
                w = wslot[pl.ds(row + (j // 2) * 256, 256), pl.ds((j % 2) * 768, 768)]
                acc = acc + nt(buf_a[j, pl.ds(r * 4, 4)].reshape(384, 768), w)
            g = acc.astype(BF16)
            if nb == 0:
                gh[rows, :] = g
            else:
                cols = pl.ds((nb - 1) * 256, 256)
                gproj[2 + nb, rows, :] = (g.astype(F32) * slope[rows, cols]).astype(BF16)

        loop(2, step)

    def gx_copy(n):
        return remote(gproj.at[n], gp2.at[n], gx_s, gx_r.at[n], d_xo)

    def gx_send(n):
        gx_copy(n).start()

    def gx_wait(n):
        gx_copy(n).wait_recv()

    joined_grad(1)
    gx_send(3)
    for l in wo_loads[0]:
        l.start()
    ag_x(1, 2)
    ag_y(1, 1)
    out_chunk(3)
    xfo.send(3)
    ag_x(1, 3)
    ag_far(1, 0)
    ro[0].relay_p()
    ro[0].relay_m()
    joined_grad(2)
    gx_send(4)
    ag_far(1, 1)
    ag_y(1, 2)
    xfo.take(0)
    joined_grad(3)
    gx_send(5)
    ro[1].relay_p()
    ro[1].relay_m()
    ag_far(1, 2)
    ag_y(1, 3)
    joined_grad(0)
    ro[2].relay_p()
    ro[2].relay_m()

    def win_load(j):
        return load(
            win.at[pl.ds(j * 768, 768), :], wslot.at[pl.ds((j % 2) * 768, 768)], 4 + j
        )

    win_load(0).start()
    win_load(1).start()

    def att_bwd(b):
        rows = pl.ds(b * 256, 256)
        for h in range(2):
            q = qkv[rows, pl.ds(h * 128, 128)]
            k = qkv[rows, pl.ds(256 + h * 128, 128)]
            v = qkv[rows, pl.ds(512 + h * 128, 128)]
            g = gh[rows, pl.ds(h * 128, 128)]
            p = pf[b * 2 + h]
            delta = jnp.sum(
                g.astype(F32) * heads[rows, pl.ds(h * 128, 128)].astype(F32),
                axis=-1, keepdims=True,
            )
            ds = (p * (nt(g, v) - delta) * SCALE).astype(BF16)
            gproj[2, rows, pl.ds(h * 128, 128)] = tn(p.astype(BF16), g).astype(BF16)
            gproj[0, rows, pl.ds(h * 128, 128)] = nn(ds, k).astype(BF16)
            gproj[1, rows, pl.ds(h * 128, 128)] = tn(ds, q).astype(BF16)

    att_bwd(0)
    att_bwd(1)
    att_bwd(2)
    gx_send(2)
    gx_send(0)
    gx_send(1)
    ag_far(1, 3)
    xfo.take(1)

    ag_drain(0)

    def transposed(o):
        ag_sib(1, o)
        j = order[o]

        def step(i):
            block = buf_b[j, pl.ds(i * 4, 4)].reshape(384, 768)
            rows = pl.ds(al(i * 384, 128), 384)
            buf_a[j, :, :, :, rows] = jnp.transpose(block).reshape(8, 2, 48, 384)

        loop(2, step)

    def in_block(n, o):
        j = order[o]
        left_own = buf_a[j, pl.ds(0, 4)].reshape(384, 768)
        left_other = buf_a[j, pl.ds(4, 4)].reshape(384, 768)
        cin[n, j] = (nn(left_own, gproj[n]) + nn(left_other, gp2[n])).astype(BF16)

    def in_finish(n):
        rn[n].arrived()
        r = rzi.at[n]
        for half, (a, b) in enumerate(((2, 5), (3, 4))):
            rows = pl.ds(half * 192, 192)
            rxi[n, rows, :] = (
                r[a].astype(F32) + r[b].astype(F32) + cin[n, z, rows, :].astype(F32)
            ).astype(BF16)

    transposed(0)
    transposed(1)
    transposed(2)
    transposed(3)
    ag_drain(1)
    gx_wait(3)
    in_block(3, 0)
    rn[3].far()
    in_block(3, 1)
    rn[3].near_p()
    in_block(3, 2)
    rn[3].near_m()
    in_block(3, 3)
    xfo.take(2)
    xfo.take(3)

    def sib_copy(j):
        return remote(buf_b.at[j, :, cn], rs_sib.at[j], m_s.at[0], ms_r.at[j], d_sib)

    def normed_grad(j):
        win_load(j).wait()
        base = (j % 2) * 768

        def step(i):
            h, n = i // 3, i % 3
            rows = pl.ds(al(h * 384, 128), 384)
            w = wslot[pl.ds(al(base + n * 256, 256), 256), :]
            acc = nt(gproj[0, rows, :], w[:, :256])
            for k in range(1, 6):
                acc = acc + nt(gproj[k, rows, :], w[:, k * 256 : k * 256 + 256])
            t = acc.astype(BF16)
            cols = pl.ds(al(n * 256, 128), 256)
            buf_b[j, pl.ds(h * 4, 4), :, :, cols] = t.reshape(4, 2, 48, 256)

        loop(6, step)
        sib_copy(j).start()
        if j < 2:
            win_load(j + 2).start()

    y_out = ((pair_p, d_yp), (pair_m, d_ym), (pair_2, d_y2))

    def sib_sum(j):
        sib_copy(j).wait_recv()

        def step(i):
            buf_b[j, i, c] = (buf_b[j, i, c].astype(F32) + rs_sib[j, i].astype(F32)).astype(BF16)

        loop(8, step)
        for i, (at, d) in enumerate(y_out):
            remote(buf_b.at[j, at, c], rs_y.at[j, i], m_s.at[1], my_r.at[j], d).start()

    def x_copy(j):
        return remote(ss_x.at[j], rs_x.at[j], m_s.at[2], mx_r.at[j], d_xn)

    def y_sum(j):
        remote(rs_y.at[j], rs_y.at[j], m_s.at[1], my_r.at[j], d_yp).wait_recv()

        def total(side):
            acc = buf_b[j, 2 * y + side, c].astype(F32)
            for i in range(3):
                acc = acc + rs_y[j, i, side].astype(F32)
            return acc

        ss_x[j] = total(xn).astype(BF16)
        x_copy(j).start()
        gn[:, pl.ds(j * 768, 768)] = total(xl)

    def x_sum(j):
        x_copy(j).wait_recv()
        cols = pl.ds(j * 768, 768)
        gn[:, cols] = gn[:, cols] + rs_x[j].astype(F32)

    normed_grad(0)
    gx_wait(4)
    in_block(4, 0)
    rn[4].far()
    in_block(4, 1)
    rn[4].near_p()
    in_block(4, 2)
    rn[4].near_m()
    in_block(4, 3)
    normed_grad(1)
    sib_sum(0)
    fo.relay_p()
    fo.relay_m()
    gx_wait(5)
    in_block(5, 0)
    rn[5].far()
    in_block(5, 1)
    rn[5].near_p()
    in_block(5, 2)
    rn[5].near_m()
    in_block(5, 3)
    rn[3].relay_p()
    rn[3].relay_m()
    normed_grad(2)
    sib_sum(1)
    rn[4].relay_p()
    rn[4].relay_m()
    co[0].send()
    co[1].send()
    gx_wait(2)
    in_block(2, 0)
    rn[2].far()
    in_block(2, 1)
    rn[2].near_p()
    in_block(2, 2)
    rn[2].near_m()
    in_block(2, 3)
    normed_grad(3)
    sib_sum(2)
    y_sum(0)
    rn[5].relay_p()
    rn[5].relay_m()
    co[2].send()
    gx_wait(0)
    in_block(0, 0)
    rn[0].far()
    in_block(0, 1)
    rn[0].near_p()
    in_block(0, 2)
    rn[0].near_m()
    in_block(0, 3)
    sib_sum(3)
    y_sum(1)
    rn[2].relay_p()
    rn[2].relay_m()
    in_finish(3)
    in_finish(4)
    xfo.finish()
    gx_wait(1)
    in_block(1, 0)
    rn[1].far()
    in_block(1, 1)
    rn[1].near_p()
    in_block(1, 2)
    rn[1].near_m()
    in_block(1, 3)
    rn[0].relay_p()
    rn[0].relay_m()
    y_sum(2)
    y_sum(3)
    in_finish(5)
    rn[1].relay_p()
    rn[1].relay_m()
    in_finish(2)
    in_finish(0)
    co[0].finish()
    co[1].finish()
    co[2].finish()
    st_o = load(rxo, gwout, 1)
    st_o.start()
    in_finish(1)
    st_i = [load(rxi.at[n], gwin.at[:, pl.ds(n * 256, 256)], 2 + n) for n in range(6)]
    for st in st_i:
        st.start()
    for j in range(4):
        x_sum(j)
    xh_v = xhat[...]
    sg = gn[...] * gain[...]
    m1 = jnp.mean(sg, axis=-1, keepdims=True)
    m2 = jnp.mean(sg * xh_v, axis=-1, keepdims=True)
    own_tok[...] = (
        own_dout[...].astype(F32) + (sg - m1 - xh_v * m2) * rstd_ref[:, :1]
    ).astype(BF16)
    st_g = load(own_tok, ig, 0)
    st_g.start()
    gx_all = remote(gproj, gp2, gx_s, gx_r.at[0], d_xo)
    gx_all.wait_send()
    nx_all().wait_send()
    for r in ro + rn + [fo] + co + [xfo]:
        r.drain()
    for b, i in ((rs_sib, 0), (rs_y, 1), (rs_x, 2)):
        remote(b, b, m_s.at[i], mx_r.at[0], d_sib).wait_send()
    st_o.wait()
    st_g.wait()
    for st in st_i:
        st.wait()


def widen(ig, gwin, gwout, ig_out, gwin_out, gwout_out, tg, ti, to, fi, fo, isem, osem):
    def copies(k):
        if k == 8:
            return ig, tg, tg, ig_out
        if k < 4:
            at = pl.ds(k * 96, 96)
            return gwin.at[at], ti.at[at], fi.at[at], gwin_out.at[at]
        at = pl.ds((k - 4) * 256, 256)
        return gwout.at[at], to.at[at], fo.at[at], gwout_out.at[at]

    ins = [pltpu.make_async_copy(copies(k)[0], copies(k)[1], isem.at[k]) for k in range(9)]
    outs = [pltpu.make_async_copy(copies(k)[2], copies(k)[3], osem.at[k]) for k in range(9)]
    for cp in ins:
        cp.start()
    for k in range(9):
        ins[k].wait()
        if k < 8:
            src, dst = copies(k)[1:3]
            dst[...] = src[...].astype(F32)
        outs[k].start()
    for cp in outs:
        cp.wait()


def body(block_input_tokens, norm_gain_vector, w_in, w_out, saved_qkv, mlp_pre, output_gradient):
    hbm = pl.BlockSpec(memory_space=pl.ANY)
    sem = pltpu.SemaphoreType.DMA
    v = pltpu.VMEM
    ig, gwin, gwout = pl.pallas_call(
        kernel,
        name="block_backward",
        out_shape=(
            jax.ShapeDtypeStruct((48, 3072), BF16),
            jax.ShapeDtypeStruct((384, 1536), BF16),
            jax.ShapeDtypeStruct((1024, 384), BF16),
        ),
        in_specs=[hbm] * 7,
        out_specs=(hbm, hbm, hbm),
        scratch_shapes=[
            v((4, 8, 2, 48, 768), BF16), v((4, 8, 2, 48, 768), BF16), v((768, 768), BF16),
            v((768, 768), BF16), v((768, 768), F32), v((6, 256, 256), F32),
            v((768, 256), BF16), v((1024, 768), BF16), v((768, 256), BF16),
            v((6, 768, 256), BF16), v((6, 768, 256), BF16), v((1536, 1536), BF16),
            v((8, 1024, 384), BF16), v((6, 4, 384, 256), BF16),
            v((NSO, 6, 2, HO, 384), BF16), v((6, 6, 192, 256), BF16),
            v((6, XO // 2, 384), BF16), v((4, XO, 384), BF16),
            v((1024, 384), BF16), v((6, 384, 256), BF16), v((4, 48, 384), BF16),
            v((4, 8, 48, 768), BF16),
            v((4, 3, 2, 48, 768), BF16), v((4, 48, 768), BF16), v((4, 48, 768), BF16),
            v((48, 3072), F32), v((48, 3072), F32), v((1, 3072), F32), v((48, 3072), BF16),
            v((48, 3072), BF16), v((48, 128), F32),
            sem((16,)), sem((2, 2)), sem((2, 5, 4)),
            sem((NSO, 6)), sem((NSO, 6)), sem((6, 6)), sem((6, 6)), sem((6,)), sem((6,)),
            sem((NSO, 2)), sem((NSO, 2)),
            sem((4,)), sem((4,)), sem, sem((6,)), sem((2,)), sem((3,)), sem((4,)), sem((4,)), sem((4,)),
        ],
        compiler_params=pltpu.CompilerParams(
            collective_id=0, has_side_effects=True, vmem_limit_bytes=63 << 20
        ),
    )(
        block_input_tokens, norm_gain_vector.reshape(1, -1), w_in, w_out, saved_qkv, mlp_pre,
        output_gradient,
    )
    return pl.pallas_call(
        widen,
        name="widen",
        out_shape=(
            jax.ShapeDtypeStruct((48, 3072), BF16),
            jax.ShapeDtypeStruct((384, 1536), F32),
            jax.ShapeDtypeStruct((1024, 384), F32),
        ),
        in_specs=[hbm] * 3,
        out_specs=(hbm,) * 3,
        scratch_shapes=[
            v((48, 3072), BF16), v((384, 1536), BF16), v((1024, 384), BF16),
            v((384, 1536), F32), v((1024, 384), F32), sem((9,)), sem((9,)),
        ],
        compiler_params=pltpu.CompilerParams(vmem_limit_bytes=62 << 20),
    )(ig, gwin, gwout)


def solution(mesh):
    placed = (
        P(("dp", "mp"), None),
        P(),
        P(None, "mp"),
        P("mp", None),
        P("dp", "mp"),
        P("dp", "mp"),
        P(("dp", "mp"), None),
    )
    return jax.shard_map(
        body,
        mesh=mesh,
        in_specs=placed,
        out_specs=(P(("dp", "mp"), None), P("dp", "mp"), P("mp", "dp")),
        check_vma=False,
    )
```
